128 devices in a mesh: inst: 8 (over z, x_lo), blk: 16 (over y, x_hi, core).
Axes of the slice: x: 4 (x_hi: 2, x_lo: 2; x = x_hi * 2 + x_lo), y: 4, z: 4, core: 2. Of those that a mesh axis runs over, the one named last changes fastest.
Arguments:
- psi_start: float32 [8, 6, 128, 8192], P('inst', None, 'blk'), may hold values from -6 to 6
- coupling: float32 [8, 6, 6], P('inst'), may hold values from -2.5 to 2.5
- center: float32 [8, 128, 8192], P('inst', 'blk'), may hold values from 4 to 8
- spread: float32 [8, 128, 8192], P('inst', 'blk'), may hold values from 0.2 to 1
- source: float32 [8, 6, 128, 8192], P('inst', None, 'blk'), may hold values from -6 to 6
- wall_geo: float32 [8, 18, 32768], P('inst', None, 'blk'), may hold values from -6 to 6
- wall_cell: int32 [32768], P('blk'), may hold values from 0 to 65535
- wall_dest: int32 [32768, 1], P('blk'), may hold values from 0 to 15; in each aligned block of 2048 rows (0 to 2047, 2048 to 4095, ...) at most 256 rows name the same one
- wall_node: int32 [32768], P('blk'), may hold values from 0 to 4095
Outputs:
- psi_out: float32 [8, 6, 128, 8192], P('inst', None, 'blk')
- sensitivity: float32 [3, 65536], P(None, 'blk')
The draws below stay inside these ranges and needn't reach their ends.
Inputs may be any that keep to these rules, and one draw needn't show every extreme that they name: `wall_dest`: among the 2048 wall faces of one grid block at most 256 go to one owner.
All inputs are finite; a program needn't handle non-finite values.
Results may differ from the reference program's by a relative error of at most 0.0001.
Values sent between devices are 32-bit elements; how exact they have to be, the bound alone decides.
No kernel may reach another device: no remote copies, remote signals or barrier semaphores. Data moves between devices by JAX's collectives and lax.ppermute only.
A program may use at most 192 MiB of HBM per device.

```python
import math
import jax
import jax.numpy as jnp
import numpy as np
from jax import lax

F = 6
XD = 8
Y = 8192
WALL_DEV = 2048
CAP = 256
NODE_DEV = 4096
ITERS = 2
INST = 8
X = 128
WALLS = 32768
NODES = 65536
N_BLK = 16


def with_ends(entries, stream_key, smallest, top_value):
    place = [jax.random.randint(jax.random.fold_in(stream_key, axis), (), 0, length) for axis, length in enumerate(entries.shape)]
    longest = entries.shape.index(max(entries.shape))
    beside = place[:longest] + [(place[longest] + 1) % entries.shape[longest]] + place[longest + 1:]
    return entries.at[tuple(place)].set(smallest).at[tuple(beside)].set(top_value)


def block_scale(rng, extent, cuts, smallest, high):
    gain, own = 1.0, jax.random.fold_in(rng, 6)
    for axis_at, parts in cuts:
        draws = jnp.exp(jax.random.uniform(jax.random.fold_in(own, axis_at), (parts,), jnp.float32, smallest / len(cuts), high / len(cuts)))
        gain = gain * jnp.repeat(draws, extent[axis_at] // parts).reshape([-1 if axis == axis_at else 1 for axis in range(len(extent))])
    return gain


def shared_out(rng, own, number, rows, count, top, most, skew):
    ranking = jax.random.permutation(rng, count)
    heavy_load, common = portions_of(count, rows * top, most, skew, True), portions_of(count, rows * top, most, skew, False)
    places = jnp.arange(count)

    def named(sizes, turn):
        used = int((sizes > 0).sum())
        fixed = max(1, used // 4)
        moved = fixed + (places - fixed + turn * (used - fixed)) % max(1, count - fixed)
        return jnp.zeros((count,), jnp.int32).at[ranking[jnp.where(places < fixed, places, moved)]].set(jnp.asarray(sizes, jnp.int32))

    sizes = jnp.where(number % 4 == 0, named(heavy_load, number // 4), named(common, number - number // 4 - 1))
    mixed = jax.random.permutation(jax.random.fold_in(own, 3), count)
    donor, taker = mixed[0:count // 2 * 2:2], mixed[1:count // 2 * 2:2]
    slack = jnp.minimum(sizes[donor] - 1, most - sizes[taker]) // 2
    slack = jnp.where((donor == ranking[0]) | (taker == ranking[0]) | (sizes[taker] == 0), 0, jnp.maximum(slack, 0))
    moved = jax.random.randint(jax.random.fold_in(own, 4), (count // 2,), 0, 1 << 20) % (slack + 1)
    sizes = sizes.at[donor].add(-moved).at[taker].add(moved)
    items = jnp.searchsorted(jnp.cumsum(sizes), jnp.arange(rows * top), side="right").astype(jnp.int32)
    grid = items.reshape(top, rows).T
    grid = grid[jax.random.permutation(jax.random.fold_in(own, 1), rows)]
    turn = jax.random.randint(jax.random.fold_in(own, 2), (rows, 1), 0, top)
    return jnp.take_along_axis(grid, (jnp.arange(top)[None, :] + turn) % top, axis=1)


def portions_of(number_of, total, limit, slope, full):
    loads = [(1 << 20) // math.isqrt(grade ** slope) + 1 for grade in range(1, number_of + 1)]
    largest = limit if full else min(limit, max(-(-total // number_of), total * loads[0] // sum(loads)))
    least = 1 if total - largest >= number_of - 1 else 0
    given, surplus = [largest] + [least] * (number_of - 1), total - largest - least * (number_of - 1)
    while surplus > 0:
        candidates = [i for i in range(1, number_of) if given[i] < largest] or [i for i in range(1, number_of) if given[i] < limit]
        mass, left = sum([loads[i] for i in candidates]), surplus
        for i in candidates:
            extra = min(limit - given[i], max(1, left * loads[i] // mass), surplus)
            given[i] = given[i] + extra
            surplus = surplus - extra
    return np.array(given)


def centred(stream_key, extent, width, limit, split=(), held_as=jnp.bfloat16):
    values = width * jax.random.normal(stream_key, extent, jnp.float32)
    if split:
        values = values * block_scale(stream_key, extent, split, -0.22, 0.18)
    return jnp.clip(values, -limit, limit).astype(held_as)


def setup_inputs(seed: int = 0) -> dict:
    arg_keys = jax.random.split(jax.random.key(seed), 10)
    psi_start = centred(arg_keys[0], (INST, F, X, Y), 1.0, 6.0, ((0, 8), (2, 16)), jnp.float32)
    coupling = centred(arg_keys[1], (INST, F, F), F ** -0.5, 2.5, ((0, 8),), jnp.float32)
    center = jnp.clip(4.0 + 4.0 * jax.random.uniform(arg_keys[2], (INST, X, Y), jnp.float32) ** block_scale(arg_keys[2], (INST, X, Y), ((0, 8), (1, 16)), -0.2, 0.2), 4.0, 8.0)
    spread = jnp.clip(jnp.exp(math.log(1.0) - 1.609438 * jax.random.uniform(arg_keys[3], (INST, X, Y), jnp.float32) ** block_scale(arg_keys[3], (INST, X, Y), ((0, 8), (1, 16)), -0.2, 0.2)), 0.2, 1.0)
    source = centred(arg_keys[4], (INST, F, X, Y), 1.0, 6.0, ((0, 8), (2, 16)), jnp.float32)
    wall_geo = centred(arg_keys[5], (INST, 3 * F, WALLS), 1.0, 6.0, ((0, 8), (2, 16)), jnp.float32)
    wall_cell = with_ends(jax.random.randint(arg_keys[6], (WALLS,), 0, XD * Y), jax.random.fold_in(arg_keys[6], 1), 0, (XD * Y) - 1).astype(jnp.int32)
    wall_dest_keys = jax.random.split(jax.random.fold_in(arg_keys[7], 1), WALLS // WALL_DEV)
    wall_dest_turns = jax.random.permutation(jax.random.fold_in(arg_keys[7], 3), WALLS // WALL_DEV)
    wall_dest = jax.vmap(lambda own, number: shared_out(jax.random.fold_in(arg_keys[7], 2), own, number, WALL_DEV, N_BLK, 1, CAP, 2))(wall_dest_keys, wall_dest_turns).reshape((WALLS, 1))
    wall_node = with_ends(jax.random.randint(arg_keys[8], (WALLS,), 0, NODE_DEV), jax.random.fold_in(arg_keys[8], 1), 0, NODE_DEV - 1).astype(jnp.int32)
    return {"psi_start": psi_start, "coupling": coupling, "center": center, "spread": spread, "source": source, "wall_geo": wall_geo, "wall_cell": wall_cell, "wall_dest": wall_dest, "wall_node": wall_node}


def spectral_matrix(count):
    index = jnp.arange(count, dtype=jnp.int32)
    offset = index[:, None] - index[None, :]
    parity = (offset % 2).astype(jnp.float32)
    same = offset == 0
    angle = jnp.pi * offset.astype(jnp.float32) / count
    safe_angle = jnp.where(same, 1.0, angle)
    values = 0.5 * (1.0 - 2.0 * parity) / jnp.sin(safe_angle)
    return jnp.where(same, 0.0, values).astype(jnp.float32)


def sweep(psi, coupling, center, spread, source, spec_mat):
    mixed = jnp.einsum("igf,igxy->ifxy", coupling, psi, precision=lax.Precision.HIGHEST)
    weighted = spread[:, None] * mixed
    beside = jnp.roll(weighted, 1, axis=2) + jnp.roll(weighted, -1, axis=2)
    padded = jnp.pad(weighted, ((0, 0), (0, 0), (0, 0), (1, 1)))
    beside = beside + padded[..., 2:] + padded[..., :-2]
    spectral = 0.5 * jnp.einsum("ji,jfxy->ifxy", spec_mat, psi, precision=lax.Precision.HIGHEST)
    update = center[:, None] * psi - beside + spectral - source
    return psi - (0.6 / center)[:, None] * update


def reference(psi_start, coupling, center, spread, source, wall_geo, wall_cell, wall_dest, wall_node):
    spec_mat = spectral_matrix(INST)
    block_of = (jnp.arange(WALLS, dtype=jnp.int32) // WALL_DEV).astype(jnp.int32)
    target = (wall_dest[:, 0] * NODE_DEV + wall_node).astype(jnp.int32)
    geometry = wall_geo.reshape(INST, 3, F, WALLS)
    sensitivity = jnp.zeros((3, NODES), jnp.float32)
    psi = psi_start
    for step in range(ITERS):
        psi = sweep(psi, coupling, center, spread, source, spec_mat)
        blocks = psi.reshape(INST, F, N_BLK, XD * Y)
        picked = blocks[:, :, block_of, wall_cell]
        partial_value = jnp.einsum("ikfe,ife->ike", geometry, picked, precision=lax.Precision.HIGHEST)
        total = jnp.sum(partial_value, axis=0)
        sensitivity = sensitivity + jax.ops.segment_sum(total.T, target, num_segments=NODES).T
    return psi, sensitivity
```

```python
import math

import jax
import jax.numpy as jnp
from jax import lax
from jax.experimental import pallas as pl
from jax.experimental.pallas import tpu as pltpu
from jax.sharding import PartitionSpec as P

CAP = 256
NODE_DEV = 4096
INST = 8
N_BLK = 16
F = 6
PLANES = 14
TILES = 8
FACES = 2048
GROUPS = FACES // 128
VMEM = 40 * 1024 * 1024

HALF_SPEC = [0.0] + [
    0.25 * (-1.0) ** d / math.sin(math.pi * d / INST) for d in range(1, INST)
]


def params():
    return pltpu.CompilerParams(vmem_limit_bytes=VMEM)


def cost(flops, nbytes):
    return pl.CostEstimate(flops=flops, bytes_accessed=nbytes, transcendentals=0)


def rows_iota(shape=(8, 128)):
    return lax.broadcasted_iota(jnp.int32, shape, 0)


def lanes_iota(shape=(8, 128)):
    return lax.broadcasted_iota(jnp.int32, shape, 1)


def full(shape):
    return pl.BlockSpec(shape, lambda *_: (0,) * len(shape))


def one(*shape):
    return pl.BlockSpec((1,) + shape, lambda i: (i,) + (0,) * len(shape))


def f32(*shape):
    return jax.ShapeDtypeStruct(shape, jnp.float32)


def pack_kernel(psi, source, center, spread, coupling, out):
    for t in range(TILES):
        cols = slice(t * 128, (t + 1) * 128)
        for f in range(F):
            out[0, t * PLANES + f] = psi[f, :, cols]
            out[0, t * PLANES + F + f] = source[f, :, cols]
        out[0, t * PLANES + 12] = 0.6 / center[:, cols]
        out[0, t * PLANES + 13] = spread[:, cols]
    out[0, TILES * PLANES] = jnp.zeros((8, 128), jnp.float32)
    out[0, TILES * PLANES, 0:F, 0:F] = coupling[0]


def pack(psi, source, center, spread, coupling):
    wide = pl.BlockSpec((F, 8, 1024), lambda c: (0, 0, c))
    flat = pl.BlockSpec((8, 1024), lambda c: (0, c))
    return pl.pallas_call(
        pack_kernel,
        grid=(INST,),
        in_specs=[wide, wide, flat, flat, full((1, F, F))],
        out_specs=one(TILES * PLANES + 1, 8, 128),
        out_shape=f32(INST, TILES * PLANES + 1, 8, 128),
        compiler_params=params(),
        cost_estimate=cost(10**6, 8 * 10**6),
    )(psi, source, center, spread, coupling)


def faces_kernel(cell, dest, chunk, list_cell, list_face, slot, count, loads):
    for owner in range(N_BLK):
        loads[owner] = 0

    def step(face, found):
        here = cell[face]
        owner = dest[face]
        rank = loads[owner]
        slot[face] = owner * CAP + rank
        loads[owner] = rank + 1
        list_cell[found] = here
        list_face[found] = face
        mine = ((here & 8191) >> 10) == chunk[0]
        return found + mine.astype(jnp.int32)

    found = lax.fori_loop(0, FACES, step, jnp.int32(0))
    count[0] = found

    def fill(at, carry):
        list_cell[at] = 0
        list_face[at] = -1
        return carry

    lax.fori_loop(found, jnp.minimum(found + 128, FACES), fill, 0)


def sort_faces(cell, dest, chunk):
    smem = pl.BlockSpec(memory_space=pltpu.SMEM)
    ints = jax.ShapeDtypeStruct((FACES,), jnp.int32)
    return pl.pallas_call(
        faces_kernel,
        in_specs=[smem] * 3,
        out_specs=[smem] * 4,
        out_shape=[ints, ints, ints, jax.ShapeDtypeStruct((1,), jnp.int32)],
        scratch_shapes=[pltpu.SMEM((N_BLK,), jnp.int32)],
        cost_estimate=cost(10**9, 10**7),
    )(cell, dest, chunk)


def fluxes(psi_of, spread_of, coupling, inner, top, bottom, left, right, held):
    row, lane = rows_iota(), lanes_iota()
    factor = [
        [jnp.broadcast_to(coupling[g : g + 1, f : f + 1], (8, 128)) for f in range(F)]
        for g in range(F)
    ]
    for t in range(TILES):
        psi = [psi_of(t, f) for f in range(F)]
        strength = spread_of(t)
        for f in range(F):
            total = factor[0][f] * psi[0]
            for g in range(1, F):
                total = total + factor[g][f] * psi[g]
            weighted = strength * total
            held[t * F + f] = weighted
            top[0, f, t : t + 1, :] = weighted[0:1, :]
            bottom[0, f, t : t + 1, :] = weighted[7:8, :]
    first = jnp.zeros((8, 128), jnp.float32)
    last = jnp.zeros((8, 128), jnp.float32)
    for f in range(F):
        tiles = [held[t * F + f] for t in range(TILES)]
        later = [pltpu.roll(x, 1, 1) for x in tiles]
        sooner = [pltpu.roll(x, 127, 1) for x in tiles]
        first = jnp.where(lane == f, jnp.broadcast_to(tiles[0][:, 0:1], (8, 128)), first)
        last = jnp.where(lane == f, jnp.broadcast_to(tiles[7][:, 127:128], (8, 128)), last)
        for t in range(TILES):
            before = later[t - 1] if t else jnp.zeros((8, 128), jnp.float32)
            after = sooner[t + 1] if t < TILES - 1 else jnp.zeros((8, 128), jnp.float32)
            total = jnp.where(lane == 0, before, later[t])
            total = total + jnp.where(lane == 127, after, sooner[t])
            total = total + jnp.where(row == 0, 0.0, pltpu.roll(tiles[t], 1, 0))
            total = total + jnp.where(row == 7, 0.0, pltpu.roll(tiles[t], 7, 0))
            inner[0, t * F + f] = total
    left[0] = first
    right[0] = last


def first_kernel(got, inner, top, bottom, left, right, scales, held):
    for t in range(TILES):
        scales[0, t] = got[0, t * PLANES + 12]
        scales[0, TILES + t] = got[0, t * PLANES + 13]
    fluxes(
        lambda t, f: got[0, t * PLANES + f],
        lambda t: got[0, t * PLANES + 13],
        got[0, TILES * PLANES],
        inner, top, bottom, left, right, held,
    )


FLUX_SPECS = [one(TILES * F, 8, 128), one(F, 8, 128), one(F, 8, 128), one(8, 128), one(8, 128)]
FLUX_SHAPES = [
    f32(INST, TILES * F, 8, 128),
    f32(INST, F, 8, 128),
    f32(INST, F, 8, 128),
    f32(INST, 8, 128),
    f32(INST, 8, 128),
]


def first_fluxes(got):
    return pl.pallas_call(
        first_kernel,
        grid=(INST,),
        in_specs=[one(TILES * PLANES + 1, 8, 128)],
        out_specs=FLUX_SPECS + [one(2 * TILES, 8, 128)],
        out_shape=FLUX_SHAPES + [f32(INST, 2 * TILES, 8, 128)],
        scratch_shapes=[pltpu.VMEM((TILES * F, 8, 128), jnp.float32)],
        compiler_params=params(),
        cost_estimate=cost(10**7, 7 * 10**6),
    )(got)


def rim(t, f, above, below, left, right):
    row, lane = rows_iota(), lanes_iota()
    total = jnp.where(row == 0, above[0, f, t : t + 1, :], 0.0)
    total = total + jnp.where(row == 7, below[0, f, t : t + 1, :], 0.0)
    if t == 0:
        total = total + jnp.where(lane == 0, jnp.broadcast_to(left[0, :, f : f + 1], (8, 128)), 0.0)
    if t == TILES - 1:
        total = total + jnp.where(lane == 127, jnp.broadcast_to(right[0, :, f : f + 1], (8, 128)), 0.0)
    return total


def second_kernel(most, scales, coupling, above, below, before, after,
                  psi, inner, top, bottom, left, right, held):
    for t in range(TILES):
        scale = scales[0, t]
        for f in range(F):
            psi[0, t * F + f] = most[0, t * F + f] + scale * rim(t, f, above, below, before, after)
    fluxes(
        lambda t, f: psi[0, t * F + f],
        lambda t: scales[0, TILES + t],
        coupling[0, 0],
        inner, top, bottom, left, right, held,
    )


HALO_SPECS = [one(F, 8, 128), one(F, 8, 128), one(8, 128), one(8, 128)]


def second_fluxes(most, scales, got, halo):
    return pl.pallas_call(
        second_kernel,
        grid=(INST,),
        in_specs=[
            one(TILES * F, 8, 128),
            one(2 * TILES, 8, 128),
            pl.BlockSpec((1, 1, 8, 128), lambda i: (i, TILES * PLANES, 0, 0)),
        ] + HALO_SPECS,
        out_specs=[one(TILES * F, 8, 128)] + FLUX_SPECS,
        out_shape=[f32(INST, TILES * F, 8, 128)] + FLUX_SHAPES,
        scratch_shapes=[pltpu.VMEM((TILES * F, 8, 128), jnp.float32)],
        compiler_params=params(),
        cost_estimate=cost(10**7, 7 * 10**6),
    )(most, scales, got, *halo)


def spectral(psi):
    def at(j):
        return (psi[j], 1) if j < INST else (psi[j - INST], -1)

    totals = []
    for i in range(INST):
        total = None
        for d in (1, 2, 3):
            (x, p), (y, q) = at(i + d), at(i + INST - d)
            pair = x + y if p == q else x - y
            sign = p
            term = (sign * HALF_SPEC[d]) * pair
            total = term if total is None else total + term
        x, p = at(i + 4)
        totals.append(total + (p * HALF_SPEC[4]) * x)
    return totals


def most_kernel(got, psi, inner, most):
    for f in range(F):
        state = [psi[i, f] for i in range(INST)]
        coupled = spectral(state)
        for i in range(INST):
            change = got[i, F + f] + inner[i, f] - coupled[i]
            most[i, f] = 0.4 * state[i] + got[i, 12] * change


def most_of_sweep(got, psi, inner):
    tile = pl.BlockSpec((INST, F, 8, 128), lambda t: (0, t, 0, 0))
    planes = pl.BlockSpec((INST, PLANES, 8, 128), lambda t: (0, t, 0, 0))
    kernel = most_kernel
    if psi is None:
        kernel = lambda got, inner, most: most_kernel(got, got, inner, most)
    return pl.pallas_call(
        kernel,
        grid=(TILES,),
        in_specs=[planes] + ([] if psi is None else [tile]) + [tile],
        out_specs=tile,
        out_shape=f32(INST, TILES * F, 8, 128),
        compiler_params=params(),
        cost_estimate=cost(10**7, 8 * 10**6),
    )(*[got] + ([] if psi is None else [psi]) + [inner])


def halos(edges):
    top, bottom, left, right = edges
    up = [(i, (i + 1) % N_BLK) for i in range(N_BLK)]
    down = [(j, i) for i, j in up]
    on = [(i, i + 1) for i in range(INST - 1)]
    back = [(j, i) for i, j in on]
    above = lax.ppermute(bottom, "blk", up)
    below = lax.ppermute(top, "blk", down)
    before = lax.ppermute(right, "inst", on)
    after = lax.ppermute(left, "inst", back)
    return above, below, before, after


def three_parts(x):
    a = x.astype(jnp.bfloat16)
    x = x - a.astype(jnp.float32)
    b = x.astype(jnp.bfloat16)
    x = x - b.astype(jnp.float32)
    return a, b, x.astype(jnp.bfloat16)


def last_kernel(count, most, psi, scales, above, below, before, after, list_cell, list_face,
                out, sums, found):
    i = pl.program_id(0)
    for t in range(TILES):
        scale = scales[0, t]
        for f in range(F):
            new = most[0, t * F + f] + scale * rim(t, f, above, below, before, after)
            out[i, t * F + f] = new
            both = new + psi[0, t * F + f]
            at = slice((t * F + f) * 8, (t * F + f) * 8 + 8)
            sums[at, :] = both
    groups = (count[0] + 127) // 128
    row = rows_iota()

    def pick(g, carry):
        cell = list_cell[pl.ds(g, 1), :]
        onehot = (rows_iota((128, 128)) == (cell & 127)).astype(jnp.bfloat16)
        lanes = jnp.concatenate([onehot] * 3, axis=0)
        state = jnp.concatenate(three_parts(sums[...]), axis=1)
        values = jnp.dot(state, lanes, preferred_element_type=jnp.float32)
        here = row == (cell >> 13)
        tile = (cell >> 7) & 7
        masks = [here & (tile == t) for t in range(TILES)]
        picked = jnp.zeros((8, 128), jnp.float32)
        for f in range(F):
            total = jnp.zeros((8, 128), jnp.float32)
            for t in range(TILES):
                at = (t * F + f) * 8
                total = jnp.where(masks[t], values[at : at + 8, :], total)
            total = jnp.sum(total, axis=0, keepdims=True)
            picked = jnp.where(row == f, total, picked)
        found[g, pl.ds(pl.multiple_of(i * 8, 8), 8), :] = picked
        return carry

    lax.fori_loop(0, groups, pick, 0)

    @pl.when(i == INST - 1)
    def _():
        for j in range(INST):
            for b in range(GROUPS):
                out[j, TILES * F + b] = jnp.zeros((8, 128), jnp.float32)

        def spread_out(g, carry):
            face = list_face[pl.ds(g, 1), :]
            parts = three_parts(found[g])
            for b in range(GROUPS):
                onehot = ((rows_iota((128, 128)) + b * 128) == face).astype(jnp.bfloat16)
                total = jnp.zeros((INST * 8, 128), jnp.float32)
                for part in parts:
                    total = total + lax.dot_general(
                        part, onehot, (((1,), (1,)), ((), ())),
                        preferred_element_type=jnp.float32)
                for j in range(INST):
                    at = TILES * F + b
                    out[j, at] = out[j, at] + total[j * 8 : j * 8 + 8, :]
            return carry

        lax.fori_loop(0, groups, spread_out, 0)


def last_state(count, most, psi, scales, halo, list_cell, list_face):
    block = one(TILES * F, 8, 128)
    faces = full((GROUPS, 128))
    shape = (INST, TILES * F + GROUPS, 8, 128)
    return pl.pallas_call(
        last_kernel,
        grid=(INST,),
        in_specs=[pl.BlockSpec(memory_space=pltpu.SMEM), block, block,
                  one(2 * TILES, 8, 128)] + HALO_SPECS + [faces, faces],
        out_specs=full(shape),
        out_shape=f32(*shape),
        scratch_shapes=[
            pltpu.VMEM((TILES * F * 8, 128), jnp.float32),
            pltpu.VMEM((GROUPS, INST * 8, 128), jnp.float32),
        ],
        compiler_params=params(),
        cost_estimate=cost(10**8, 7 * 10**6),
    )(count, most, psi, scales, *halo, list_cell.reshape(GROUPS, 128), list_face.reshape(GROUPS, 128))


def unpack_kernel(got, psi):
    for t in range(TILES):
        for f in range(F):
            psi[0, f, :, t * 128 : (t + 1) * 128] = got[0, t * F + f]


def unpack(got):
    return pl.pallas_call(
        unpack_kernel,
        grid=(INST,),
        in_specs=[one(TILES * F + GROUPS, 8, 128)],
        out_specs=pl.BlockSpec((1, F, 8, 1024), lambda c: (0, 0, 0, c)),
        out_shape=f32(1, F, 8, 8192),
        compiler_params=params(),
        cost_estimate=cost(10**6, 4 * 10**6),
    )(got)


def slots_kernel(got, geometry, slot, node, out):
    row = rows_iota()
    total = jnp.zeros((N_BLK * 8, 128), jnp.float32)
    for b in range(GROUPS):
        cols = slice(b * 128, (b + 1) * 128)
        picked = got[0, b]
        for c in range(1, INST):
            picked = picked + got[c, b]
        values = jnp.broadcast_to(node[:, cols].astype(jnp.float32), (8, 128))
        for k in range(3):
            part = jnp.sum(geometry[k * F : (k + 1) * F, cols] * picked[0:F, :], axis=0, keepdims=True)
            values = jnp.where((row >> 1) == k, part, values)
        place = slot[:, cols]
        half = (row & 1) == ((place >> 7) & 1)
        owner = place >> 8
        values = jnp.where(half, values, 0.0)
        rows = jnp.concatenate(
            [jnp.where(owner == d, values, 0.0) for d in range(N_BLK)], axis=0)
        onehot = (rows_iota((128, 128)) == (place & 127)).astype(jnp.bfloat16)
        for part in three_parts(rows):
            total = total + lax.dot_general(
                part, onehot, (((1,), (1,)), ((), ())), preferred_element_type=jnp.float32)
    for i in range(INST):
        for d in range(N_BLK):
            out[i * N_BLK + d] = total[d * 8 : d * 8 + 8, :]


def pack_slots(got, geometry, slot, node):
    return pl.pallas_call(
        slots_kernel,
        grid=(1,),
        in_specs=[pl.BlockSpec((INST, GROUPS, 8, 128), lambda _: (0, 3, 0, 0)),
                  full((3 * F, FACES)), full((1, FACES)), full((1, FACES))],
        out_specs=full((INST * N_BLK, 8, 128)),
        out_shape=f32(INST * N_BLK, 8, 128),
        compiler_params=params(),
        cost_estimate=cost(10**8, 2 * 10**6),
    )(got, geometry, slot.reshape(1, FACES), node.reshape(1, FACES))


def nodes_kernel(got, out):
    total = jnp.zeros((96, 128), jnp.float32)
    for b in range(N_BLK):
        values = got[b]
        for i in range(1, INST):
            values = values + got[i * N_BLK + b]
        nodes = got[b].astype(jnp.int32)
        for half in range(2):
            node = nodes[6 + half : 7 + half, :]
            high = rows_iota((32, 128)) == (node >> 7)
            rows = jnp.concatenate(
                [jnp.where(high, values[k * 2 + half : k * 2 + half + 1, :], 0.0) for k in range(3)],
                axis=0)
            onehot = (rows_iota((128, 128)) == (node & 127)).astype(jnp.bfloat16)
            for part in three_parts(rows):
                total = total + lax.dot_general(
                    part, onehot, (((1,), (1,)), ((), ())), preferred_element_type=jnp.float32)
    for k in range(3):
        for h in range(32):
            out[k : k + 1, h * 128 : (h + 1) * 128] = total[k * 32 + h : k * 32 + h + 1, :]


def to_nodes(got):
    return pl.pallas_call(
        nodes_kernel,
        in_specs=[pl.BlockSpec(memory_space=pltpu.VMEM)],
        out_specs=pl.BlockSpec(memory_space=pltpu.VMEM),
        out_shape=f32(3, NODE_DEV),
        compiler_params=params(),
        cost_estimate=cost(10**8, 10**6),
    )(got)


def local(psi_start, coupling, center, spread, source, wall_geo, wall_cell, wall_dest, wall_node):
    chunk = lax.axis_index("inst").astype(jnp.int32).reshape(1)
    sent = pack(psi_start[0], source[0], center[0], spread[0], coupling)
    got = lax.all_to_all(sent, "inst", 0, 0, tiled=True)
    list_cell, list_face, slot, count = sort_faces(wall_cell, wall_dest[:, 0], chunk)

    inner, *edges, scales = first_fluxes(got)
    halo = halos(edges)
    most = most_of_sweep(got, None, inner)
    psi, inner, *edges = second_fluxes(most, scales, got, halo)
    halo = halos(edges)
    most = most_of_sweep(got, psi, inner)
    back = last_state(count, most, psi, scales, halo, list_cell, list_face)

    home = lax.all_to_all(back, "inst", 0, 0, tiled=True)
    slots = pack_slots(home, wall_geo[0], slot, wall_node)
    owned = lax.all_to_all(slots, ("inst", "blk"), 0, 0, tiled=True)
    return unpack(home), to_nodes(owned)


def solution(mesh):
    placed = (
        P("inst", None, "blk", None),
        P("inst", None, None),
        P("inst", "blk", None),
        P("inst", "blk", None),
        P("inst", None, "blk", None),
        P("inst", None, "blk"),
        P("blk"),
        P("blk", None),
        P("blk"),
    )
    return jax.shard_map(
        local,
        mesh=mesh,
        in_specs=placed,
        out_specs=(P("inst", None, "blk", None), P(None, "blk")),
        check_vma=False,
    )
```

```python
import math

import jax
import jax.numpy as jnp
from jax import lax
from jax.experimental import pallas as pl
from jax.experimental.pallas import tpu as pltpu
from jax.sharding import PartitionSpec as P

CAP = 256
NODE_DEV = 4096
INST = 8
N_BLK = 16
F = 6
PLANES = 14
TILES = 8
FACES = 2048
GROUPS = FACES // 128
VMEM = 16 * 1024 * 1024
SENT = TILES * PLANES + 1

HALF_SPEC = [0.0] + [
    0.25 * (-1.0) ** d / math.sin(math.pi * d / INST) for d in range(1, INST)
]


def params(limit=VMEM):
    return pltpu.CompilerParams(vmem_limit_bytes=limit)


def cost(flops, nbytes):
    return pl.CostEstimate(flops=flops, bytes_accessed=nbytes, transcendentals=0)


def rows_iota(shape=(8, 128)):
    return lax.broadcasted_iota(jnp.int32, shape, 0)


def lanes_iota(shape=(8, 128)):
    return lax.broadcasted_iota(jnp.int32, shape, 1)


def full(shape):
    return pl.BlockSpec(shape, lambda *_: (0,) * len(shape))


def one(*shape):
    return pl.BlockSpec((1,) + shape, lambda i: (i,) + (0,) * len(shape))


def f32(*shape):
    return jax.ShapeDtypeStruct(shape, jnp.float32)


def tiled(x):
    x = x.reshape(x.shape[:-1] + (INST * TILES, 128))
    return jnp.swapaxes(x, -3, -2)


def pack_kernel(flip, psi, source, center, spread, coupling, out, flat, held, sems, more):
    def tiles_of(d):
        return pl.ds((d ^ flip[0]) * TILES, TILES)

    def load(d, n):
        start = (psi if n < F else source).at[n % F, tiles_of(d)]
        return pltpu.make_async_copy(start, held.at[d, pl.ds(n * TILES, TILES)], sems.at[d, n])

    def send(d):
        return pltpu.make_async_copy(held.at[d], out.at[d], more.at[2 + d])

    flats = [
        pltpu.make_async_copy(center, flat.at[0], more.at[0]),
        pltpu.make_async_copy(spread, flat.at[1], more.at[1]),
    ]
    for copy in flats:
        copy.start()
    for d in range(INST):
        for n in range(2 * F):
            load(d, n).start()
    for copy in flats:
        copy.wait()
    for d in range(INST):
        at = 2 * F * TILES
        held[d, at : at + TILES] = 0.6 / flat[0, tiles_of(d)]
        held[d, at + TILES : at + 2 * TILES] = flat[1, tiles_of(d)]
        held[d, SENT - 1] = jnp.zeros((8, 128), jnp.float32)
        held[d, SENT - 1, 0:F, 0:F] = coupling[0]
        for n in range(2 * F):
            load(d, n).wait()
        send(d).start()
    for d in range(INST):
        send(d).wait()


def pack(psi, source, center, spread, coupling, flip):
    vmem = pl.BlockSpec(memory_space=pltpu.VMEM)
    anywhere = pl.BlockSpec(memory_space=pl.ANY)
    return pl.pallas_call(
        pack_kernel,
        in_specs=[pl.BlockSpec(memory_space=pltpu.SMEM)] + [anywhere] * 4 + [vmem],
        out_specs=anywhere,
        out_shape=f32(INST, SENT, 8, 128),
        scratch_shapes=[
            pltpu.VMEM((2, INST * TILES, 8, 128), jnp.float32),
            pltpu.VMEM((INST, SENT, 8, 128), jnp.float32),
            pltpu.SemaphoreType.DMA((INST, 2 * F)),
            pltpu.SemaphoreType.DMA((2 + INST,)),
        ],
        compiler_params=params(60 * 1024 * 1024),
        cost_estimate=cost(10**6, 8 * 10**6),
    )(flip, tiled(psi), tiled(source), tiled(center), tiled(spread), coupling)


def faces_kernel(cell, dest, chunk, list_cell, list_face, slot, count, loads):
    for owner in range(N_BLK):
        loads[owner] = 0

    def step(face, found):
        here = cell[face]
        owner = dest[face]
        rank = loads[owner]
        slot[face] = owner * CAP + rank
        loads[owner] = rank + 1
        list_cell[found] = here
        list_face[found] = face
        mine = ((here & 8191) >> 10) == chunk[0]
        return found + mine.astype(jnp.int32)

    found = lax.fori_loop(0, FACES, step, jnp.int32(0))
    count[0] = found

    def fill(at, carry):
        list_cell[at] = 0
        list_face[at] = -1
        return carry

    lax.fori_loop(found, jnp.minimum(found + 128, FACES), fill, 0)


def sort_faces(cell, dest, chunk):
    smem = pl.BlockSpec(memory_space=pltpu.SMEM)
    ints = jax.ShapeDtypeStruct((FACES,), jnp.int32)
    return pl.pallas_call(
        faces_kernel,
        in_specs=[smem] * 3,
        out_specs=[smem] * 4,
        out_shape=[ints, ints, ints, jax.ShapeDtypeStruct((1,), jnp.int32)],
        scratch_shapes=[pltpu.SMEM((N_BLK,), jnp.int32)],
        compiler_params=pltpu.CompilerParams(vmem_limit_bytes=2**20),
        cost_estimate=cost(10**9, 10**7),
    )(cell, dest, chunk)


def fluxes(i, psi_of, spread_of, coupling, inner, top, bottom, left, right, held):
    row, lane = rows_iota(), lanes_iota()
    factor = [
        [jnp.broadcast_to(coupling[g : g + 1, f : f + 1], (8, 128)) for f in range(F)]
        for g in range(F)
    ]
    for t in range(TILES):
        psi = [psi_of(t, f) for f in range(F)]
        strength = spread_of(t)
        for f in range(F):
            total = factor[0][f] * psi[0]
            for g in range(1, F):
                total = total + factor[g][f] * psi[g]
            weighted = strength * total
            held[f * TILES + t] = weighted
            top[i, f, t : t + 1, :] = weighted[0:1, :]
            bottom[i, f, t : t + 1, :] = weighted[7:8, :]
    first = jnp.zeros((8, 128), jnp.float32)
    last = jnp.zeros((8, 128), jnp.float32)
    for f in range(F):
        tiles = [held[f * TILES + t] for t in range(TILES)]
        later = [pltpu.roll(x, 1, 1) for x in tiles]
        sooner = [pltpu.roll(x, 127, 1) for x in tiles]
        first = jnp.where(lane == f, jnp.broadcast_to(tiles[0][:, 0:1], (8, 128)), first)
        last = jnp.where(lane == f, jnp.broadcast_to(tiles[7][:, 127:128], (8, 128)), last)
        for t in range(TILES):
            before = later[t - 1] if t else jnp.zeros((8, 128), jnp.float32)
            after = sooner[t + 1] if t < TILES - 1 else jnp.zeros((8, 128), jnp.float32)
            total = jnp.where(lane == 0, before, later[t])
            total = total + jnp.where(lane == 127, after, sooner[t])
            total = total + jnp.where(row == 0, 0.0, pltpu.roll(tiles[t], 1, 0))
            total = total + jnp.where(row == 7, 0.0, pltpu.roll(tiles[t], 7, 0))
            inner[i, f * TILES + t] = total
    left[i] = first
    right[i] = last


def first_kernel(got, inner, top, bottom, left, right, psi, source, scales, held, sems):
    def loads(i, n):
        at = (0, F * TILES, 2 * F * TILES)[n]
        to = (psi, source, scales)[n]
        return pltpu.make_async_copy(got.at[i, pl.ds(at, to.shape[1])], to.at[i], sems.at[n, i])

    for i in range(INST):
        loads(i, 0).start()
        loads(i, 2).start()
    for i in range(INST):
        loads(i, 1).start()

    def step(i, carry):
        loads(i, 0).wait()
        loads(i, 2).wait()
        fluxes(
            i,
            lambda t, f: psi[i, f * TILES + t],
            lambda t: scales[i, TILES + t],
            scales[i, 2 * TILES],
            inner, top, bottom, left, right, held,
        )
        return carry

    lax.fori_loop(0, INST, step, 0)
    for i in range(INST):
        loads(i, 1).wait()


FLUX_SPECS = [one(TILES * F, 8, 128), one(F, 8, 128), one(F, 8, 128), one(8, 128), one(8, 128)]
FLUX_SHAPES = [
    f32(INST, TILES * F, 8, 128),
    f32(INST, F, 8, 128),
    f32(INST, F, 8, 128),
    f32(INST, 8, 128),
    f32(INST, 8, 128),
]


def first_fluxes(got):
    vmem = pl.BlockSpec(memory_space=pltpu.VMEM)
    state = f32(INST, TILES * F, 8, 128)
    return pl.pallas_call(
        first_kernel,
        in_specs=[pl.BlockSpec(memory_space=pl.ANY)],
        out_specs=[vmem] * 8,
        out_shape=FLUX_SHAPES + [state, state, f32(INST, 2 * TILES + 1, 8, 128)],
        scratch_shapes=[
            pltpu.VMEM((TILES * F, 8, 128), jnp.float32),
            pltpu.SemaphoreType.DMA((3, INST)),
        ],
        compiler_params=params(),
        cost_estimate=cost(10**7, 7 * 10**6),
    )(got)


def rim(t, f, above, below, left, right):
    row, lane = rows_iota(), lanes_iota()
    total = jnp.where(row == 0, above[0, f, t : t + 1, :], 0.0)
    total = total + jnp.where(row == 7, below[0, f, t : t + 1, :], 0.0)
    if t == 0:
        total = total + jnp.where(lane == 0, jnp.broadcast_to(left[0, :, f : f + 1], (8, 128)), 0.0)
    if t == TILES - 1:
        total = total + jnp.where(lane == 127, jnp.broadcast_to(right[0, :, f : f + 1], (8, 128)), 0.0)
    return total


def second_kernel(most, scales, above, below, before, after,
                  psi, inner, top, bottom, left, right, held):
    for t in range(TILES):
        scale = scales[0, t]
        for f in range(F):
            psi[0, f * TILES + t] = most[0, f * TILES + t] + scale * rim(t, f, above, below, before, after)
    fluxes(
        0,
        lambda t, f: psi[0, f * TILES + t],
        lambda t: scales[0, TILES + t],
        scales[0, 2 * TILES],
        inner, top, bottom, left, right, held,
    )


HALO_SPECS = [one(F, 8, 128), one(F, 8, 128), one(8, 128), one(8, 128)]


def second_fluxes(most, scales, halo):
    return pl.pallas_call(
        second_kernel,
        grid=(INST,),
        in_specs=[
            one(TILES * F, 8, 128),
            one(2 * TILES + 1, 8, 128),
        ] + HALO_SPECS,
        out_specs=[one(TILES * F, 8, 128)] + FLUX_SPECS,
        out_shape=[f32(INST, TILES * F, 8, 128)] + FLUX_SHAPES,
        scratch_shapes=[pltpu.VMEM((TILES * F, 8, 128), jnp.float32)],
        compiler_params=params(),
        cost_estimate=cost(10**7, 7 * 10**6),
    )(most, scales, *halo)


def spectral(psi):
    def at(j):
        return (psi[j], 1) if j < INST else (psi[j - INST], -1)

    totals = []
    for i in range(INST):
        total = None
        for d in (1, 2, 3):
            (x, p), (y, q) = at(i + d), at(i + INST - d)
            pair = x + y if p == q else x - y
            sign = p
            term = (sign * HALF_SPEC[d]) * pair
            total = term if total is None else total + term
        x, p = at(i + 4)
        totals.append(total + (p * HALF_SPEC[4]) * x)
    return totals


def most_kernel(psi, source, scale, inner, most):
    for t in range(TILES):
        state = [psi[i, t] for i in range(INST)]
        coupled = spectral(state)
        for i in range(INST):
            change = source[i, t] + inner[i, t] - coupled[i]
            most[i, t] = 0.4 * state[i] + scale[i, t] * change


def most_of_sweep(psi, source, scales, inner):
    field = pl.BlockSpec((INST, TILES, 8, 128), lambda f: (0, f, 0, 0))
    scale = pl.BlockSpec((INST, TILES, 8, 128), lambda f: (0, 0, 0, 0))
    return pl.pallas_call(
        most_kernel,
        grid=(F,),
        in_specs=[field, field, scale, field],
        out_specs=field,
        out_shape=f32(INST, TILES * F, 8, 128),
        compiler_params=params(),
        cost_estimate=cost(10**7, 8 * 10**6),
    )(psi, source, scales, inner)


def device(chunk, block):
    return (chunk ^ ((block >> 1) & 1)) * N_BLK + block


def halos(edges):
    top, bottom, left, right = edges
    axes = ("inst", "blk")
    places = [(c, b) for c in range(INST) for b in range(N_BLK)]
    up = [(device(c, b), device(c, (b + 1) % N_BLK)) for c, b in places]
    down = [(j, i) for i, j in up]
    on = [(device(c, b), device(c + 1, b)) for c, b in places if c + 1 < INST]
    back = [(j, i) for i, j in on]
    above = lax.ppermute(bottom, axes, up)
    below = lax.ppermute(top, axes, down)
    before = lax.ppermute(right, axes, on)
    after = lax.ppermute(left, axes, back)
    return above, below, before, after


def stacked(x):
    return jnp.concatenate(three_parts(x), axis=0)


def times_transposed(x, y):
    return lax.dot_general(x, y, (((1,), (1,)), ((), ())), preferred_element_type=jnp.float32)


def three_parts(x):
    a = x.astype(jnp.bfloat16)
    x = x - a.astype(jnp.float32)
    b = x.astype(jnp.bfloat16)
    x = x - b.astype(jnp.float32)
    return a, b, x.astype(jnp.bfloat16)


def last_kernel(count, faces, most, psi, scales, above, below, before, after, list_cell, list_face,
                out, *sums):
    i = pl.program_id(0)
    both = [[] for f in range(F)]
    for t in range(TILES):
        scale = scales[0, t]
        for f in range(F):
            new = most[0, f * TILES + t] + scale * rim(t, f, above, below, before, after)
            out[i, f * TILES + t] = new
            both[f].append(new + psi[0, f * TILES + t])
            if t % 2:
                rows = slice((f * TILES + t - 1) * 8, (f * TILES + t + 1) * 8)
                for part, value in zip(sums, three_parts(jnp.concatenate(both[f][-2:], axis=0))):
                    part[i, rows, :] = value

    @pl.when(i == INST - 1)
    def _():
        groups = (count[0] + 127) // 128
        row = rows_iota()
        for j in range(INST):
            for b in range(GROUPS):
                out[j, TILES * F + b] = jnp.zeros((8, 128), jnp.float32)

        def pick(g, carry):
            cell = list_cell[pl.ds(g, 1), :]
            onehot = (rows_iota((128, 128)) == (cell & 127)).astype(jnp.bfloat16)
            here = row == (cell >> 13)
            tile = (cell >> 7) & 7
            masks = [here & (tile == t) for t in range(TILES)]
            found = []
            for j in range(INST):
                taken = sum(
                    jnp.dot(part[j], onehot, preferred_element_type=jnp.float32) for part in sums)
                picked = jnp.zeros((8, 128), jnp.float32)
                for f in range(F):
                    total = jnp.zeros((8, 128), jnp.float32)
                    for t in range(TILES):
                        at = (f * TILES + t) * 8
                        total = jnp.where(masks[t], taken[at : at + 8, :], total)
                    total = jnp.sum(total, axis=0, keepdims=True)
                    picked = jnp.where(row == f, total, picked)
                found.append(picked)
            parts = jnp.concatenate(three_parts(jnp.concatenate(found, axis=0)), axis=0)
            face = list_face[pl.ds(g, 1), :]
            last = jnp.minimum(g * 128 + 127, count[0] - 1)

            def place(b, carry):
                onehot = ((rows_iota((128, 128)) + b * 128) == face).astype(jnp.bfloat16)
                total = lax.dot_general(
                    parts, onehot, (((1,), (1,)), ((), ())), preferred_element_type=jnp.float32)
                at = TILES * F + b
                for j in range(INST):
                    rows = [total[n : n + 8, :] for n in (j * 8, 64 + j * 8, 128 + j * 8)]
                    out[j, at] = out[j, at] + (rows[0] + rows[1] + rows[2])
                return carry

            lax.fori_loop(faces[g * 128] >> 7, (faces[last] >> 7) + 1, place, 0)
            return carry

        lax.fori_loop(0, groups, pick, 0)


def last_state(count, most, psi, scales, halo, list_cell, list_face):
    block = one(TILES * F, 8, 128)
    faces = full((GROUPS, 128))
    shape = (INST, TILES * F + GROUPS, 8, 128)
    return pl.pallas_call(
        last_kernel,
        grid=(INST,),
        in_specs=[pl.BlockSpec(memory_space=pltpu.SMEM)] * 2 + [block, block,
                  one(2 * TILES, 8, 128)] + HALO_SPECS + [faces, faces],
        out_specs=full(shape),
        out_shape=f32(*shape),
        scratch_shapes=[pltpu.VMEM((INST, TILES * F * 8, 128), jnp.bfloat16)] * 3,
        compiler_params=params(),
        cost_estimate=cost(10**8, 7 * 10**6),
    )(count, list_face, most, psi, scales, *halo, list_cell.reshape(GROUPS, 128), list_face.reshape(GROUPS, 128))


def unpack_kernel(flip, got, psi):
    for t in range(TILES):
        for f in range(F):
            psi[0, f, :, t * 128 : (t + 1) * 128] = got[0, f * TILES + t]


def unpack(got, flip):
    return pl.pallas_call(
        unpack_kernel,
        grid_spec=pltpu.PrefetchScalarGridSpec(
            num_scalar_prefetch=1,
            grid=(INST,),
            in_specs=[pl.BlockSpec((1, TILES * F, 8, 128), lambda d, flip: (d, 0, 0, 0))],
            out_specs=pl.BlockSpec((1, F, 8, 1024), lambda d, flip: (0, 0, 0, d ^ flip[0])),
        ),
        out_shape=f32(1, F, 8, 8192),
        compiler_params=params(),
        cost_estimate=cost(10**6, 4 * 10**6),
    )(flip, got)


def slots_kernel(got, geometry, slot, node, out):
    row = rows_iota()
    total = jnp.zeros((3 * N_BLK * 8, 128), jnp.float32)
    for b in range(GROUPS):
        cols = slice(b * 128, (b + 1) * 128)
        picked = got[0, b]
        for c in range(1, INST):
            picked = picked + got[c, b]
        values = jnp.broadcast_to(node[:, cols].astype(jnp.float32), (8, 128))
        for k in range(3):
            part = jnp.sum(geometry[k * F : (k + 1) * F, cols] * picked[0:F, :], axis=0, keepdims=True)
            values = jnp.where((row >> 1) == k, part, values)
        place = slot[:, cols]
        half = (row & 1) == ((place >> 7) & 1)
        owner = place >> 8
        values = jnp.where(half, values, 0.0)
        rows = jnp.concatenate(
            [jnp.where(owner == d, values, 0.0) for d in range(N_BLK)], axis=0)
        onehot = (rows_iota((128, 128)) == (place & 127)).astype(jnp.bfloat16)
        total = total + times_transposed(stacked(rows), onehot)
    total = total[0:128] + total[128:256] + total[256:384]
    for i in range(INST):
        for d in range(N_BLK):
            out[i * N_BLK + d] = total[d * 8 : d * 8 + 8, :]


def pack_slots(got, geometry, slot, node):
    return pl.pallas_call(
        slots_kernel,
        grid=(1,),
        in_specs=[pl.BlockSpec((INST, GROUPS, 8, 128), lambda _: (0, 3, 0, 0)),
                  full((3 * F, FACES)), full((1, FACES)), full((1, FACES))],
        out_specs=full((INST * N_BLK, 8, 128)),
        out_shape=f32(INST * N_BLK, 8, 128),
        compiler_params=params(),
        cost_estimate=cost(10**8, 2 * 10**6),
    )(got, geometry, slot.reshape(1, FACES), node.reshape(1, FACES))


def nodes_kernel(got, out):
    total = jnp.zeros((3 * 96, 128), jnp.float32)
    for b in range(N_BLK):
        values = got[b]
        for i in range(1, INST):
            values = values + got[i * N_BLK + b]
        nodes = got[b].astype(jnp.int32)
        for half in range(2):
            node = nodes[6 + half : 7 + half, :]
            high = rows_iota((32, 128)) == (node >> 7)
            rows = jnp.concatenate(
                [jnp.where(high, values[k * 2 + half : k * 2 + half + 1, :], 0.0) for k in range(3)],
                axis=0)
            onehot = (rows_iota((128, 128)) == (node & 127)).astype(jnp.bfloat16)
            total = total + times_transposed(stacked(rows), onehot)
    total = total[0:96] + total[96:192] + total[192:288]
    for k in range(3):
        for h in range(32):
            out[k : k + 1, h * 128 : (h + 1) * 128] = total[k * 32 + h : k * 32 + h + 1, :]


def to_nodes(got):
    return pl.pallas_call(
        nodes_kernel,
        in_specs=[pl.BlockSpec(memory_space=pltpu.VMEM)],
        out_specs=pl.BlockSpec(memory_space=pltpu.VMEM),
        out_shape=f32(3, NODE_DEV),
        compiler_params=params(),
        cost_estimate=cost(10**8, 10**6),
    )(got)


def local(psi_start, coupling, center, spread, source, wall_geo, wall_cell, wall_dest, wall_node):
    flip = ((lax.axis_index("blk").astype(jnp.int32) >> 1) & 1).reshape(1)
    chunk = lax.axis_index("inst").astype(jnp.int32).reshape(1) ^ flip
    sent = pack(psi_start[0], source[0], center[0], spread[0], coupling, flip)
    got = lax.all_to_all(sent, "inst", 0, 0, tiled=True)
    faces = sort_faces(wall_cell, wall_dest[:, 0], chunk)
    got, (list_cell, list_face, slot, count) = lax.optimization_barrier((got, faces))

    inner, *edges, psi, source, scales = first_fluxes(got)
    halo = halos(edges)
    most = most_of_sweep(psi, source, scales, inner)
    psi, inner, *edges = second_fluxes(most, scales, halo)
    halo = halos(edges)
    most = most_of_sweep(psi, source, scales, inner)
    back = last_state(count, most, psi, scales, halo, list_cell, list_face)

    home = lax.all_to_all(back, "inst", 0, 0, tiled=True)
    slots = pack_slots(home, wall_geo[0], slot, wall_node)
    owned = lax.all_to_all(slots, ("inst", "blk"), 0, 0, tiled=True)
    return unpack(home, flip), to_nodes(owned)


def solution(mesh):
    placed = (
        P("inst", None, "blk", None),
        P("inst", None, None),
        P("inst", "blk", None),
        P("inst", "blk", None),
        P("inst", None, "blk", None),
        P("inst", None, "blk"),
        P("blk"),
        P("blk", None),
        P("blk"),
    )
    return jax.shard_map(
        local,
        mesh=mesh,
        in_specs=placed,
        out_specs=(P("inst", None, "blk", None), P(None, "blk")),
        check_vma=False,
    )
```

```python
import math

import jax
import jax.numpy as jnp
from jax import lax
from jax.experimental import pallas as pl
from jax.experimental.pallas import tpu as pltpu
from jax.sharding import PartitionSpec as P

CAP = 256
NODE_DEV = 4096
INST = 8
N_BLK = 16
F = 6
TILES = 8
FACES = 2048
GROUPS = FACES // 128
PACKED = GROUPS * F // 8
VMEM = 16 * 1024 * 1024
STATE = F * TILES
SENT = STATE + 2 * TILES + 1

HALF_SPEC = [0.0] + [
    0.25 * (-1.0) ** d / math.sin(math.pi * d / INST) for d in range(1, INST)
]


def params(limit=VMEM):
    return pltpu.CompilerParams(vmem_limit_bytes=limit)


def cost(flops, nbytes):
    return pl.CostEstimate(flops=flops, bytes_accessed=nbytes, transcendentals=0)


def rows_iota(shape=(8, 128)):
    return lax.broadcasted_iota(jnp.int32, shape, 0)


def lanes_iota(shape=(8, 128)):
    return lax.broadcasted_iota(jnp.int32, shape, 1)


def full(shape):
    return pl.BlockSpec(shape, lambda *_: (0,) * len(shape))


def one(*shape):
    return pl.BlockSpec((1,) + shape, lambda i: (i,) + (0,) * len(shape))


def f32(*shape):
    return jax.ShapeDtypeStruct(shape, jnp.float32)


def tiled(x):
    x = x.reshape(x.shape[:-1] + (INST * TILES, 128))
    return jnp.swapaxes(x, -3, -2)


def tiles_of(d, flip):
    return pl.ds((d ^ flip[0]) * TILES, TILES)


def pack_kernel(flip, psi, center, spread, coupling, out, flat, held, sems, more):
    def load(d, f):
        start = psi.at[f, tiles_of(d, flip)]
        return pltpu.make_async_copy(start, held.at[d, pl.ds(f * TILES, TILES)], sems.at[d, f])

    def send(d):
        return pltpu.make_async_copy(held.at[d], out.at[d], more.at[2 + d])

    flats = [
        pltpu.make_async_copy(center, flat.at[0], more.at[0]),
        pltpu.make_async_copy(spread, flat.at[1], more.at[1]),
    ]
    for copy in flats:
        copy.start()
    for d in range(INST):
        for f in range(F):
            load(d, f).start()
    for copy in flats:
        copy.wait()
    for d in range(INST):
        held[d, STATE : STATE + TILES] = 0.6 / flat[0, tiles_of(d, flip)]
        held[d, STATE + TILES : STATE + 2 * TILES] = flat[1, tiles_of(d, flip)]
        held[d, SENT - 1] = jnp.zeros((8, 128), jnp.float32)
        for g in range(F):
            held[d, SENT - 1, g : g + 1, 0:F] = coupling[g]
        for f in range(F):
            load(d, f).wait()
        send(d).start()
    for d in range(INST):
        send(d).wait()


def pack(psi, center, spread, coupling, flip):
    vmem = pl.BlockSpec(memory_space=pltpu.VMEM)
    anywhere = pl.BlockSpec(memory_space=pl.ANY)
    return pl.pallas_call(
        pack_kernel,
        in_specs=[pl.BlockSpec(memory_space=pltpu.SMEM)] + [anywhere] * 3 + [vmem],
        out_specs=anywhere,
        out_shape=f32(INST, SENT, 8, 128),
        scratch_shapes=[
            pltpu.VMEM((2, INST * TILES, 8, 128), jnp.float32),
            pltpu.VMEM((INST, SENT, 8, 128), jnp.float32),
            pltpu.SemaphoreType.DMA((INST, F)),
            pltpu.SemaphoreType.DMA((2 + INST,)),
        ],
        compiler_params=params(60 * 1024 * 1024),
        cost_estimate=cost(10**6, 5 * 10**6),
    )(flip, tiled(psi), tiled(center), tiled(spread), jnp.swapaxes(coupling, 0, 1))


def pack_source_kernel(flip, source, out, held, sems, more):
    def load(d, f):
        start = source.at[f, tiles_of(d, flip)]
        return pltpu.make_async_copy(start, held.at[d, pl.ds(f * TILES, TILES)], sems.at[d, f])

    def send(d):
        return pltpu.make_async_copy(held.at[d], out.at[d], more.at[d])

    for d in range(INST):
        for f in range(F):
            load(d, f).start()
    for d in range(INST):
        for f in range(F):
            load(d, f).wait()
        send(d).start()
    for d in range(INST):
        send(d).wait()


def pack_source(source, flip):
    anywhere = pl.BlockSpec(memory_space=pl.ANY)
    return pl.pallas_call(
        pack_source_kernel,
        in_specs=[pl.BlockSpec(memory_space=pltpu.SMEM), anywhere],
        out_specs=anywhere,
        out_shape=f32(INST, STATE, 8, 128),
        scratch_shapes=[
            pltpu.VMEM((INST, STATE, 8, 128), jnp.float32),
            pltpu.SemaphoreType.DMA((INST, F)),
            pltpu.SemaphoreType.DMA((INST,)),
        ],
        compiler_params=params(60 * 1024 * 1024),
        cost_estimate=cost(10**6, 4 * 10**6),
    )(flip, tiled(source))


def faces_kernel(cell, dest, chunk, list_cell, list_face, slot, count, loads):
    for owner in range(N_BLK):
        loads[owner] = 0

    def step(face, found):
        here = cell[face]
        owner = dest[face]
        rank = loads[owner]
        slot[face] = owner * CAP + rank
        loads[owner] = rank + 1
        list_cell[found] = here
        list_face[found] = face
        mine = ((here & 8191) >> 10) == chunk[0]
        return found + mine.astype(jnp.int32)

    found = lax.fori_loop(0, FACES, step, jnp.int32(0))
    count[0] = found

    def fill(at, carry):
        list_cell[at] = 0
        list_face[at] = -1
        return carry

    lax.fori_loop(found, jnp.minimum(found + 128, FACES), fill, 0)


def sort_faces(cell, dest, chunk):
    smem = pl.BlockSpec(memory_space=pltpu.SMEM)
    ints = jax.ShapeDtypeStruct((FACES,), jnp.int32)
    return pl.pallas_call(
        faces_kernel,
        in_specs=[smem] * 3,
        out_specs=[smem] * 4,
        out_shape=[ints, ints, ints, jax.ShapeDtypeStruct((1,), jnp.int32)],
        scratch_shapes=[pltpu.SMEM((N_BLK,), jnp.int32)],
        compiler_params=pltpu.CompilerParams(vmem_limit_bytes=2**20),
        cost_estimate=cost(10**9, 10**7),
    )(cell, dest, chunk)


def fluxes(i, side, psi_of, spread_of, coupling, inner, near, far, near_side, far_side, held):
    row, lane = rows_iota(), lanes_iota()
    factor = [
        [jnp.broadcast_to(coupling[g : g + 1, f : f + 1], (8, 128)) for f in range(F)]
        for g in range(F)
    ]
    for t in range(TILES):
        psi = [psi_of(t, f) for f in range(F)]
        strength = spread_of(t)
        for f in range(F):
            total = factor[0][f] * psi[0]
            for g in range(1, F):
                total = total + factor[g][f] * psi[g]
            weighted = strength * total
            held[f * TILES + t] = weighted
            top, bottom = weighted[0:1, :], weighted[7:8, :]
            near[i, f, t : t + 1, :] = jnp.where(side[0] == 1, top, bottom)
            far[i, f, t : t + 1, :] = jnp.where(side[0] == 1, bottom, top)
    first = jnp.zeros((8, 128), jnp.float32)
    last = jnp.zeros((8, 128), jnp.float32)
    for f in range(F):
        tiles = [held[f * TILES + t] for t in range(TILES)]
        later = [pltpu.roll(x, 1, 1) for x in tiles]
        sooner = [pltpu.roll(x, 127, 1) for x in tiles]
        first = jnp.where(lane == f, jnp.broadcast_to(tiles[0][:, 0:1], (8, 128)), first)
        last = jnp.where(lane == f, jnp.broadcast_to(tiles[7][:, 127:128], (8, 128)), last)
        for t in range(TILES):
            before = later[t - 1] if t else jnp.zeros((8, 128), jnp.float32)
            after = sooner[t + 1] if t < TILES - 1 else jnp.zeros((8, 128), jnp.float32)
            total = jnp.where(lane == 0, before, later[t])
            total = total + jnp.where(lane == 127, after, sooner[t])
            total = total + jnp.where(row == 0, 0.0, pltpu.roll(tiles[t], 1, 0))
            total = total + jnp.where(row == 7, 0.0, pltpu.roll(tiles[t], 7, 0))
            inner[i, f * TILES + t] = total
    near_side[i] = jnp.where(side[1] == 1, first, last)
    far_side[i] = jnp.where(side[1] == 1, last, first)


FLUX_SHAPES = [
    f32(INST, STATE, 8, 128),
    f32(INST, F, 8, 128),
    f32(INST, F, 8, 128),
    f32(INST, 8, 128),
    f32(INST, 8, 128),
]


def first_kernel(side, got, inner, near, far, near_side, far_side, psi, scales, held, sems):
    def loads(i, n):
        to = (psi, scales)[n]
        start = got.at[i, pl.ds(n * STATE, to.shape[1])]
        return pltpu.make_async_copy(start, to.at[i], sems.at[n, i])

    for i in range(INST):
        loads(i, 0).start()
        loads(i, 1).start()

    def step(i, carry):
        loads(i, 0).wait()
        loads(i, 1).wait()
        fluxes(
            i, side,
            lambda t, f: psi[i, f * TILES + t],
            lambda t: scales[i, TILES + t],
            scales[i, 2 * TILES],
            inner, near, far, near_side, far_side, held,
        )
        return carry

    lax.fori_loop(0, INST, step, 0)


def first_fluxes(side, got):
    vmem = pl.BlockSpec(memory_space=pltpu.VMEM)
    return pl.pallas_call(
        first_kernel,
        in_specs=[pl.BlockSpec(memory_space=pltpu.SMEM), pl.BlockSpec(memory_space=pl.ANY)],
        out_specs=[vmem] * 7,
        out_shape=FLUX_SHAPES + [f32(INST, STATE, 8, 128), f32(INST, 2 * TILES + 1, 8, 128)],
        scratch_shapes=[
            pltpu.VMEM((STATE, 8, 128), jnp.float32),
            pltpu.SemaphoreType.DMA((2, INST)),
        ],
        compiler_params=params(),
        cost_estimate=cost(10**7, 7 * 10**6),
    )(side, got)


def rim(i, t, f, side, near, far, near_side, far_side):
    row, lane = rows_iota(), lanes_iota()
    near_row = jnp.where(side[0] == 1, 0, 7)
    total = jnp.where(row == near_row, near[i, f, t : t + 1, :], 0.0)
    total = total + jnp.where(row == 7 - near_row, far[i, f, t : t + 1, :], 0.0)
    if t == 0:
        left = jnp.where(side[1] == 1, near_side[i], far_side[i])
        total = total + jnp.where(lane == 0, jnp.broadcast_to(left[:, f : f + 1], (8, 128)), 0.0)
    if t == TILES - 1:
        right = jnp.where(side[1] == 1, far_side[i], near_side[i])
        total = total + jnp.where(lane == 127, jnp.broadcast_to(right[:, f : f + 1], (8, 128)), 0.0)
    return total


def second_kernel(side, got, most, scales, a, b, c, d,
                  psi, source, inner, near, far, near_side, far_side, held, sems):
    def load(i):
        return pltpu.make_async_copy(got.at[i], source.at[i], sems.at[i])

    for i in range(INST):
        load(i).start()

    def step(i, carry):
        load(i).wait()
        for t in range(TILES):
            scale = scales[i, t]
            for f in range(F):
                at = f * TILES + t
                psi[i, at] = most[i, at] + scale * (source[i, at] + rim(i, t, f, side, a, b, c, d))
        fluxes(
            i, side,
            lambda t, f: psi[i, f * TILES + t],
            lambda t: scales[i, TILES + t],
            scales[i, 2 * TILES],
            inner, near, far, near_side, far_side, held,
        )
        return carry

    lax.fori_loop(0, INST, step, 0)


HALO_SPECS = [one(F, 8, 128), one(F, 8, 128), one(8, 128), one(8, 128)]


def second_fluxes(side, got, most, scales, halo):
    vmem = pl.BlockSpec(memory_space=pltpu.VMEM)
    state = f32(INST, STATE, 8, 128)
    return pl.pallas_call(
        second_kernel,
        in_specs=[pl.BlockSpec(memory_space=pltpu.SMEM), pl.BlockSpec(memory_space=pl.ANY)] + [vmem] * 6,
        out_specs=[vmem] * 7,
        out_shape=[state, state] + FLUX_SHAPES,
        scratch_shapes=[
            pltpu.VMEM((STATE, 8, 128), jnp.float32),
            pltpu.SemaphoreType.DMA((INST,)),
        ],
        compiler_params=params(),
        cost_estimate=cost(10**7, 7 * 10**6),
    )(side, got, most, scales, *halo)


def spectral(psi):
    def at(j):
        return (psi[j], 1) if j < INST else (psi[j - INST], -1)

    totals = []
    for i in range(INST):
        total = None
        for d in (1, 2, 3):
            (x, p), (y, q) = at(i + d), at(i + INST - d)
            pair = x + y if p == q else x - y
            sign = p
            term = (sign * HALF_SPEC[d]) * pair
            total = term if total is None else total + term
        x, p = at(i + 4)
        totals.append(total + (p * HALF_SPEC[4]) * x)
    return totals


def most_kernel(psi, scale, inner, *rest):
    most = rest[-1]
    for t in range(TILES):
        state = [psi[i, t] for i in range(INST)]
        coupled = spectral(state)
        for i in range(INST):
            change = inner[i, t] - coupled[i]
            if len(rest) > 1:
                change = change + rest[0][i, t]
            most[i, t] = 0.4 * state[i] + scale[i, t] * change


def most_of_sweep(psi, scales, inner, *source):
    field = pl.BlockSpec((INST, TILES, 8, 128), lambda f: (0, f, 0, 0))
    scale = pl.BlockSpec((INST, TILES, 8, 128), lambda f: (0, 0, 0, 0))
    return pl.pallas_call(
        most_kernel,
        grid=(F,),
        in_specs=[field, scale, field] + [field] * len(source),
        out_specs=field,
        out_shape=f32(INST, STATE, 8, 128),
        compiler_params=params(),
        cost_estimate=cost(10**7, 8 * 10**6),
    )(psi, scales, inner, *source)


def device(chunk, block):
    return (chunk ^ ((block >> 1) & 1)) * N_BLK + block


def halos(edges):
    near, far, near_side, far_side = edges
    axes = ("inst", "blk")
    places = [(c, b) for c in range(INST) for b in range(N_BLK)]
    in_pair = [(device(c, b), device(c, b ^ 1)) for c, b in places]
    across = [
        (device(c, b), device(c, (b + 2 * (b % 2) - 1) % N_BLK)) for c, b in places]
    sides_in_pair = [(device(c, b), device(c ^ 1, b)) for c, b in places]
    sides_across = [
        (device(c, b), device(c + 2 * (c % 2) - 1, b))
        for c, b in places if 0 < c < INST - 1]
    return (
        lax.ppermute(near, axes, in_pair),
        lax.ppermute(far, axes, across),
        lax.ppermute(near_side, axes, sides_in_pair),
        lax.ppermute(far_side, axes, sides_across),
    )


def stacked(x):
    return jnp.concatenate(two_parts(x), axis=0)


def times_transposed(x, y):
    return lax.dot_general(x, y, (((1,), (1,)), ((), ())), preferred_element_type=jnp.float32)


def two_parts(x):
    a = x.astype(jnp.bfloat16)
    return a, (x - a.astype(jnp.float32)).astype(jnp.bfloat16)


def last_kernel(count, faces, side, most, psi, scales, a, b, c, d, list_cell, list_face,
                out, placed, *sums):
    i = pl.program_id(0)
    both = [[] for f in range(F)]
    for t in range(TILES):
        scale = scales[0, t]
        for f in range(F):
            new = most[0, f * TILES + t] + scale * rim(0, t, f, side, a, b, c, d)
            out[i, f * TILES + t] = new
            both[f].append(new + psi[0, f * TILES + t])
            if t % 2:
                rows = slice((f * TILES + t - 1) * 8, (f * TILES + t + 1) * 8)
                for part, value in zip(sums, two_parts(jnp.concatenate(both[f][-2:], axis=0))):
                    part[i, rows, :] = value

    @pl.when(i == INST - 1)
    def _():
        groups = (count[0] + 127) // 128
        row = rows_iota()
        placed[...] = jnp.zeros_like(placed)

        def pick(g, carry):
            cell = list_cell[pl.ds(g, 1), :]
            onehot = (rows_iota((128, 128)) == (cell & 127)).astype(jnp.bfloat16)
            here = row == (cell >> 13)
            tile = (cell >> 7) & 7
            masks = [here & (tile == t) for t in range(TILES)]
            found = []
            for j in range(INST):
                taken = sum(
                    jnp.dot(part[j], onehot, preferred_element_type=jnp.float32) for part in sums)
                picked = jnp.zeros((8, 128), jnp.float32)
                for f in range(F):
                    total = jnp.zeros((8, 128), jnp.float32)
                    for t in range(TILES):
                        at = (f * TILES + t) * 8
                        total = jnp.where(masks[t], taken[at : at + 8, :], total)
                    total = jnp.sum(total, axis=0, keepdims=True)
                    picked = jnp.where(row == f, total, picked)
                found.append(picked)
            parts = stacked(jnp.concatenate(found, axis=0))
            face = list_face[pl.ds(g, 1), :]
            last = jnp.minimum(g * 128 + 127, count[0] - 1)

            def place(b, carry):
                onehot = ((rows_iota((128, 128)) + b * 128) == face).astype(jnp.bfloat16)
                total = lax.dot_general(
                    parts, onehot, (((1,), (1,)), ((), ())), preferred_element_type=jnp.float32)
                for j in range(INST):
                    rows = [total[n : n + 8, :] for n in (j * 8, 64 + j * 8)]
                    placed[j, b] = placed[j, b] + (rows[0] + rows[1])
                return carry

            lax.fori_loop(faces[g * 128] >> 7, (faces[last] >> 7) + 1, place, 0)
            return carry

        lax.fori_loop(0, groups, pick, 0)
        for j in range(INST):
            for b in range(PACKED):
                rest = pltpu.roll(placed[j, PACKED + b // 3], 6 - 2 * (b % 3), 0)
                out[j, STATE + b] = jnp.where(row < F, placed[j, b], rest)


def last_state(count, side, most, psi, scales, halo, list_cell, list_face):
    block = one(STATE, 8, 128)
    faces = full((GROUPS, 128))
    shape = (INST, STATE + PACKED, 8, 128)
    return pl.pallas_call(
        last_kernel,
        grid=(INST,),
        in_specs=[pl.BlockSpec(memory_space=pltpu.SMEM)] * 3 + [block, block,
                  one(2 * TILES, 8, 128)] + HALO_SPECS + [faces, faces],
        out_specs=full(shape),
        out_shape=f32(*shape),
        scratch_shapes=[pltpu.VMEM((INST, GROUPS, 8, 128), jnp.float32)]
        + [pltpu.VMEM((INST, STATE * 8, 128), jnp.bfloat16)] * 2,
        compiler_params=params(),
        cost_estimate=cost(10**8, 7 * 10**6),
    )(count, list_face, side, most, psi, scales, *halo, list_cell.reshape(GROUPS, 128), list_face.reshape(GROUPS, 128))


def unpack_kernel(flip, got, psi):
    for t in range(TILES):
        for f in range(F):
            psi[0, f, :, t * 128 : (t + 1) * 128] = got[0, f * TILES + t]


def unpack(got, flip):
    return pl.pallas_call(
        unpack_kernel,
        grid_spec=pltpu.PrefetchScalarGridSpec(
            num_scalar_prefetch=1,
            grid=(INST,),
            in_specs=[pl.BlockSpec((1, STATE, 8, 128), lambda d, flip: (d, 0, 0, 0))],
            out_specs=pl.BlockSpec((1, F, 8, 1024), lambda d, flip: (0, 0, 0, d ^ flip[0])),
        ),
        out_shape=f32(1, F, 8, 8192),
        compiler_params=params(),
        cost_estimate=cost(10**6, 4 * 10**6),
    )(flip, got)


def slots_kernel(got, geometry, slot, node, out):
    row = rows_iota()
    total = jnp.zeros((2 * N_BLK * 8, 128), jnp.float32)
    sums = []
    for b in range(PACKED):
        picked = got[0, b]
        for c in range(1, INST):
            picked = picked + got[c, b]
        sums.append(picked)
    for q in range(GROUPS - PACKED):
        picked = pltpu.roll(sums[3 * q], 2, 0)
        for m in (1, 2):
            rest = pltpu.roll(sums[3 * q + m], 2 + 2 * m, 0)
            picked = jnp.where((row >> 1) == m, rest, picked)
        sums.append(picked)
    for b in range(GROUPS):
        cols = slice(b * 128, (b + 1) * 128)
        picked = sums[b]
        values = jnp.broadcast_to(node[:, cols].astype(jnp.float32), (8, 128))
        for k in range(3):
            part = jnp.sum(geometry[k * F : (k + 1) * F, cols] * picked[0:F, :], axis=0, keepdims=True)
            values = jnp.where((row >> 1) == k, part, values)
        place = slot[:, cols]
        half = (row & 1) == ((place >> 7) & 1)
        owner = place >> 8
        values = jnp.where(half, values, 0.0)
        rows = jnp.concatenate(
            [jnp.where(owner == d, values, 0.0) for d in range(N_BLK)], axis=0)
        onehot = (rows_iota((128, 128)) == (place & 127)).astype(jnp.bfloat16)
        total = total + times_transposed(stacked(rows), onehot)
    total = total[0:128] + total[128:256]
    for i in range(INST):
        for d in range(N_BLK):
            out[i * N_BLK + d] = total[d * 8 : d * 8 + 8, :]


def pack_slots(got, geometry, slot, node):
    return pl.pallas_call(
        slots_kernel,
        grid=(1,),
        in_specs=[pl.BlockSpec((INST, PACKED, 8, 128), lambda _: (0, STATE // PACKED, 0, 0)),
                  full((3 * F, FACES)), full((1, FACES)), full((1, FACES))],
        out_specs=full((INST * N_BLK, 8, 128)),
        out_shape=f32(INST * N_BLK, 8, 128),
        compiler_params=params(),
        cost_estimate=cost(10**8, 2 * 10**6),
    )(got, geometry, slot.reshape(1, FACES), node.reshape(1, FACES))


def nodes_kernel(got, out):
    total = jnp.zeros((2 * 96, 128), jnp.float32)
    for b in range(N_BLK):
        values = got[b]
        for i in range(1, INST):
            values = values + got[i * N_BLK + b]
        nodes = got[b].astype(jnp.int32)
        for half in range(2):
            node = nodes[6 + half : 7 + half, :]
            high = rows_iota((32, 128)) == (node >> 7)
            rows = jnp.concatenate(
                [jnp.where(high, values[k * 2 + half : k * 2 + half + 1, :], 0.0) for k in range(3)],
                axis=0)
            onehot = (rows_iota((128, 128)) == (node & 127)).astype(jnp.bfloat16)
            total = total + times_transposed(stacked(rows), onehot)
    total = total[0:96] + total[96:192]
    for k in range(3):
        for h in range(32):
            out[k : k + 1, h * 128 : (h + 1) * 128] = total[k * 32 + h : k * 32 + h + 1, :]


def to_nodes(got):
    return pl.pallas_call(
        nodes_kernel,
        in_specs=[pl.BlockSpec(memory_space=pltpu.VMEM)],
        out_specs=pl.BlockSpec(memory_space=pltpu.VMEM),
        out_shape=f32(3, NODE_DEV),
        compiler_params=params(),
        cost_estimate=cost(10**8, 10**6),
    )(got)


def local(psi_start, coupling, center, spread, source, wall_geo, wall_cell, wall_dest, wall_node):
    block = lax.axis_index("blk").astype(jnp.int32)
    flip = ((block >> 1) & 1).reshape(1)
    chunk = lax.axis_index("inst").astype(jnp.int32).reshape(1) ^ flip
    side = jnp.concatenate([(block & 1).reshape(1), chunk & 1])

    got = lax.all_to_all(
        pack(psi_start[0], center[0], spread[0], coupling, flip), "inst", 0, 0, tiled=True)
    faces = sort_faces(wall_cell, wall_dest[:, 0], chunk)
    sent = pack_source(source[0], flip)
    got, sent, (list_cell, list_face, slot, count) = lax.optimization_barrier((got, sent, faces))
    got_source = lax.all_to_all(sent, "inst", 0, 0, tiled=True)

    inner, *edges, psi, scales = first_fluxes(side, got)
    halo = halos(edges)
    most = most_of_sweep(psi, scales, inner)
    psi, source, inner, *edges = second_fluxes(side, got_source, most, scales, halo)
    halo = halos(edges)
    most = most_of_sweep(psi, scales, inner, source)
    back = last_state(count, side, most, psi, scales, halo, list_cell, list_face)

    home = lax.all_to_all(back, "inst", 0, 0, tiled=True)
    slots = pack_slots(home, wall_geo[0], slot, wall_node)
    owned = lax.all_to_all(slots, ("inst", "blk"), 0, 0, tiled=True)
    return unpack(home, flip), to_nodes(owned)


def solution(mesh):
    placed = (
        P("inst", None, "blk", None),
        P("inst", None, None),
        P("inst", "blk", None),
        P("inst", "blk", None),
        P("inst", None, "blk", None),
        P("inst", None, "blk"),
        P("blk"),
        P("blk", None),
        P("blk"),
    )
    return jax.shard_map(
        local,
        mesh=mesh,
        in_specs=placed,
        out_specs=(P("inst", None, "blk", None), P(None, "blk")),
        check_vma=False,
    )
```

```python
import math

import jax
import jax.numpy as jnp
from jax import lax
from jax.experimental import pallas as pl
from jax.experimental.pallas import tpu as pltpu
from jax.sharding import PartitionSpec as P

CAP = 256
NODE_DEV = 4096
INST = 8
N_BLK = 16
F = 6
TILES = 8
FACES = 2048
GROUPS = FACES // 128
PACKED = GROUPS * F // 8
VMEM = 16 * 1024 * 1024
STATE = F * TILES
SENT = STATE + 2 * TILES + 1

HALF_SPEC = [0.0] + [
    0.25 * (-1.0) ** d / math.sin(math.pi * d / INST) for d in range(1, INST)
]


def params(limit=VMEM):
    return pltpu.CompilerParams(vmem_limit_bytes=limit)


def cost(flops, nbytes):
    return pl.CostEstimate(flops=flops, bytes_accessed=nbytes, transcendentals=0)


def rows_iota(shape=(8, 128)):
    return lax.broadcasted_iota(jnp.int32, shape, 0)


def lanes_iota(shape=(8, 128)):
    return lax.broadcasted_iota(jnp.int32, shape, 1)


def full(shape):
    return pl.BlockSpec(shape, lambda *_: (0,) * len(shape))


def one(*shape):
    return pl.BlockSpec((1,) + shape, lambda i: (i,) + (0,) * len(shape))


def f32(*shape):
    return jax.ShapeDtypeStruct(shape, jnp.float32)


def tiled(x):
    x = x.reshape(x.shape[:-1] + (INST * TILES, 128))
    return jnp.swapaxes(x, -3, -2)


def flipped():
    return (lax.axis_index("blk").astype(jnp.int32) >> 1) & 1


def sides():
    chunk = lax.axis_index("inst").astype(jnp.int32) ^ flipped()
    return lax.axis_index("blk").astype(jnp.int32) & 1, chunk & 1


def tiles_of(d, flip):
    return pl.ds((d ^ flip) * TILES, TILES)


def pack_kernel(psi, center, spread, coupling, out, flat, factors, held, sems, more):
    flip = flipped()

    def load(d, f):
        start = psi.at[f, tiles_of(d, flip)]
        return pltpu.make_async_copy(start, held.at[d, pl.ds(f * TILES, TILES)], sems.at[d, f])

    def send(d):
        return pltpu.make_async_copy(held.at[d], out.at[d], more.at[2 + d])

    flats = [
        pltpu.make_async_copy(coupling, factors, more.at[2 + INST]),
        pltpu.make_async_copy(center, flat.at[0], more.at[0]),
        pltpu.make_async_copy(spread, flat.at[1], more.at[1]),
    ]
    for copy in flats:
        copy.start()
    for d in range(INST):
        for f in range(F):
            load(d, f).start()
    for copy in flats:
        copy.wait()
    for d in range(INST):
        held[d, STATE : STATE + TILES] = 0.6 / flat[0, tiles_of(d, flip)]
        held[d, STATE + TILES : STATE + 2 * TILES] = flat[1, tiles_of(d, flip)]
        held[d, SENT - 1] = jnp.zeros((8, 128), jnp.float32)
        for g in range(F):
            held[d, SENT - 1, g : g + 1, 0:F] = factors[g]
        for f in range(F):
            load(d, f).wait()
        send(d).start()
    for d in range(INST):
        send(d).wait()


def pack(psi, center, spread, coupling):
    anywhere = pl.BlockSpec(memory_space=pl.ANY)
    return pl.pallas_call(
        pack_kernel,
        in_specs=[anywhere] * 4,
        out_specs=anywhere,
        out_shape=f32(INST, SENT, 8, 128),
        scratch_shapes=[
            pltpu.VMEM((2, INST * TILES, 8, 128), jnp.float32),
            pltpu.VMEM((F, 1, F), jnp.float32),
            pltpu.VMEM((INST, SENT, 8, 128), jnp.float32),
            pltpu.SemaphoreType.DMA((INST, F)),
            pltpu.SemaphoreType.DMA((3 + INST,)),
        ],
        compiler_params=params(60 * 1024 * 1024),
        cost_estimate=cost(10**6, 5 * 10**6),
    )(tiled(psi), tiled(center), tiled(spread), jnp.swapaxes(coupling, 0, 1))


def pack_source_kernel(source, out, held, sems, more):
    flip = flipped()

    def load(d, f):
        start = source.at[f, tiles_of(d, flip)]
        return pltpu.make_async_copy(start, held.at[d, pl.ds(f * TILES, TILES)], sems.at[d, f])

    def send(d):
        return pltpu.make_async_copy(held.at[d], out.at[d], more.at[d])

    for d in range(INST):
        for f in range(F):
            load(d, f).start()
    for d in range(INST):
        for f in range(F):
            load(d, f).wait()
        send(d).start()
    for d in range(INST):
        send(d).wait()


def pack_source(source):
    anywhere = pl.BlockSpec(memory_space=pl.ANY)
    return pl.pallas_call(
        pack_source_kernel,
        in_specs=[anywhere],
        out_specs=anywhere,
        out_shape=f32(INST, STATE, 8, 128),
        scratch_shapes=[
            pltpu.VMEM((INST, STATE, 8, 128), jnp.float32),
            pltpu.SemaphoreType.DMA((INST, F)),
            pltpu.SemaphoreType.DMA((INST,)),
        ],
        compiler_params=params(60 * 1024 * 1024),
        cost_estimate=cost(10**6, 4 * 10**6),
    )(tiled(source))


def faces_kernel(cell, dest, chunk, list_cell, list_face, slot, count, loads):
    for owner in range(N_BLK):
        loads[owner] = 0

    def step(face, found):
        here = cell[face]
        owner = dest[face]
        rank = loads[owner]
        slot[face] = owner * CAP + rank
        loads[owner] = rank + 1
        list_cell[found] = here
        list_face[found] = face
        mine = ((here & 8191) >> 10) == chunk[0]
        return found + mine.astype(jnp.int32)

    found = lax.fori_loop(0, FACES, step, jnp.int32(0))
    count[0] = found

    def fill(at, carry):
        list_cell[at] = 0
        list_face[at] = -1
        return carry

    lax.fori_loop(found, jnp.minimum(found + 128, FACES), fill, 0)


def sort_faces(cell, dest, chunk):
    smem = pl.BlockSpec(memory_space=pltpu.SMEM)
    ints = jax.ShapeDtypeStruct((FACES,), jnp.int32)
    return pl.pallas_call(
        faces_kernel,
        in_specs=[smem] * 3,
        out_specs=[smem] * 4,
        out_shape=[ints, ints, ints, jax.ShapeDtypeStruct((1,), jnp.int32)],
        scratch_shapes=[pltpu.SMEM((N_BLK,), jnp.int32)],
        compiler_params=pltpu.CompilerParams(vmem_limit_bytes=2**20),
        cost_estimate=cost(10**9, 10**7),
    )(cell, dest, chunk)


def fluxes(i, side, psi_of, spread_of, coupling, inner, near, far, near_side, far_side, held):
    row, lane = rows_iota(), lanes_iota()
    factor = [
        [jnp.broadcast_to(coupling[g : g + 1, f : f + 1], (8, 128)) for f in range(F)]
        for g in range(F)
    ]
    for t in range(TILES):
        psi = [psi_of(t, f) for f in range(F)]
        strength = spread_of(t)
        for f in range(F):
            total = factor[0][f] * psi[0]
            for g in range(1, F):
                total = total + factor[g][f] * psi[g]
            weighted = strength * total
            at = (f * TILES + t) * 8
            held[at : at + 8, :] = weighted
    near_row = jnp.where(side[0] == 1, 0, 7)
    first = jnp.zeros((8, 128), jnp.float32)
    last = jnp.zeros((8, 128), jnp.float32)
    for f in range(F):
        near[i, f] = held[pl.ds(f * TILES * 8 + near_row, TILES, stride=8), :]
        far[i, f] = held[pl.ds(f * TILES * 8 + 7 - near_row, TILES, stride=8), :]
        tiles = [held[(f * TILES + t) * 8 : (f * TILES + t + 1) * 8, :] for t in range(TILES)]
        later = [pltpu.roll(x, 1, 1) for x in tiles]
        sooner = [pltpu.roll(x, 127, 1) for x in tiles]
        first = jnp.where(lane == f, jnp.broadcast_to(tiles[0][:, 0:1], (8, 128)), first)
        last = jnp.where(lane == f, jnp.broadcast_to(tiles[7][:, 127:128], (8, 128)), last)
        for t in range(TILES):
            before = later[t - 1] if t else jnp.zeros((8, 128), jnp.float32)
            after = sooner[t + 1] if t < TILES - 1 else jnp.zeros((8, 128), jnp.float32)
            total = jnp.where(lane == 0, before, later[t])
            total = total + jnp.where(lane == 127, after, sooner[t])
            total = total + jnp.where(row == 0, 0.0, pltpu.roll(tiles[t], 1, 0))
            total = total + jnp.where(row == 7, 0.0, pltpu.roll(tiles[t], 7, 0))
            inner[i, f * TILES + t] = total
    near_side[i] = jnp.where(side[1] == 1, first, last)
    far_side[i] = jnp.where(side[1] == 1, last, first)


FLUX_SHAPES = [
    f32(INST, STATE, 8, 128),
    f32(INST, F, 8, 128),
    f32(INST, F, 8, 128),
    f32(INST, 8, 128),
    f32(INST, 8, 128),
]


def first_kernel(got, inner, near, far, near_side, far_side, psi, scales, held, sems):
    side = sides()

    def loads(i, n):
        to = (psi, scales)[n]
        start = got.at[i, pl.ds(n * STATE, to.shape[1])]
        return pltpu.make_async_copy(start, to.at[i], sems.at[n, i])

    for i in range(INST):
        loads(i, 0).start()
        loads(i, 1).start()

    def step(i, carry):
        loads(i, 0).wait()
        loads(i, 1).wait()
        fluxes(
            i, side,
            lambda t, f: psi[i, f * TILES + t],
            lambda t: scales[i, TILES + t],
            scales[i, 2 * TILES],
            inner, near, far, near_side, far_side, held,
        )
        return carry

    lax.fori_loop(0, INST, step, 0)


def first_fluxes(got):
    vmem = pl.BlockSpec(memory_space=pltpu.VMEM)
    return pl.pallas_call(
        first_kernel,
        in_specs=[pl.BlockSpec(memory_space=pl.ANY)],
        out_specs=[vmem] * 7,
        out_shape=FLUX_SHAPES + [f32(INST, STATE, 8, 128), f32(INST, 2 * TILES + 1, 8, 128)],
        scratch_shapes=[
            pltpu.VMEM((STATE * 8, 128), jnp.float32),
            pltpu.SemaphoreType.DMA((2, INST)),
        ],
        compiler_params=params(),
        cost_estimate=cost(10**7, 7 * 10**6),
    )(got)


def rim(i, t, f, side, near, far, near_side, far_side):
    row, lane = rows_iota(), lanes_iota()
    near_row = jnp.where(side[0] == 1, 0, 7)
    total = jnp.where(row == near_row, near[i, f, t : t + 1, :], 0.0)
    total = total + jnp.where(row == 7 - near_row, far[i, f, t : t + 1, :], 0.0)
    if t == 0:
        left = jnp.where(side[1] == 1, near_side[i], far_side[i])
        total = total + jnp.where(lane == 0, jnp.broadcast_to(left[:, f : f + 1], (8, 128)), 0.0)
    if t == TILES - 1:
        right = jnp.where(side[1] == 1, far_side[i], near_side[i])
        total = total + jnp.where(lane == 127, jnp.broadcast_to(right[:, f : f + 1], (8, 128)), 0.0)
    return total


def second_kernel(got, most, scales, a, b, c, d,
                  psi, source, inner, near, far, near_side, far_side, held, sems):
    side = sides()

    def load(i):
        return pltpu.make_async_copy(got.at[i], source.at[i], sems.at[i])

    for i in range(2):
        load(i).start()

    def step(i, carry):
        load(i).wait()

        @pl.when(i + 2 < INST)
        def _():
            load(i + 2).start()

        for t in range(TILES):
            scale = scales[i, t]
            for f in range(F):
                at = f * TILES + t
                psi[i, at] = most[i, at] + scale * (source[i, at] + rim(i, t, f, side, a, b, c, d))
        fluxes(
            i, side,
            lambda t, f: psi[i, f * TILES + t],
            lambda t: scales[i, TILES + t],
            scales[i, 2 * TILES],
            inner, near, far, near_side, far_side, held,
        )
        return carry

    lax.fori_loop(0, INST, step, 0)


HALO_SPECS = [one(F, 8, 128), one(F, 8, 128), one(8, 128), one(8, 128)]


def second_fluxes(got, most, scales, halo):
    vmem = pl.BlockSpec(memory_space=pltpu.VMEM)
    state = f32(INST, STATE, 8, 128)
    return pl.pallas_call(
        second_kernel,
        in_specs=[pl.BlockSpec(memory_space=pl.ANY)] + [vmem] * 6,
        out_specs=[vmem] * 7,
        out_shape=[state, state] + FLUX_SHAPES,
        scratch_shapes=[
            pltpu.VMEM((STATE * 8, 128), jnp.float32),
            pltpu.SemaphoreType.DMA((INST,)),
        ],
        compiler_params=params(),
        cost_estimate=cost(10**7, 7 * 10**6),
    )(got, most, scales, *halo)


def spectral(psi):
    def at(j):
        return (psi[j], 1) if j < INST else (psi[j - INST], -1)

    totals = []
    for i in range(INST):
        total = None
        for d in (1, 2, 3):
            (x, p), (y, q) = at(i + d), at(i + INST - d)
            pair = x + y if p == q else x - y
            sign = p
            term = (sign * HALF_SPEC[d]) * pair
            total = term if total is None else total + term
        x, p = at(i + 4)
        totals.append(total + (p * HALF_SPEC[4]) * x)
    return totals


def most_kernel(psi, scale, inner, *rest):
    most = rest[-1]
    for t in range(TILES):
        state = [psi[i, t] for i in range(INST)]
        coupled = spectral(state)
        for i in range(INST):
            change = inner[i, t] - coupled[i]
            if len(rest) > 1:
                change = change + rest[0][i, t]
            most[i, t] = 0.4 * state[i] + scale[i, t] * change


def most_of_sweep(psi, scales, inner, *source):
    field = pl.BlockSpec((INST, TILES, 8, 128), lambda f: (0, f, 0, 0))
    scale = pl.BlockSpec((INST, TILES, 8, 128), lambda f: (0, 0, 0, 0))
    return pl.pallas_call(
        most_kernel,
        grid=(F,),
        in_specs=[field, scale, field] + [field] * len(source),
        out_specs=field,
        out_shape=f32(INST, STATE, 8, 128),
        compiler_params=params(),
        cost_estimate=cost(10**7, 8 * 10**6),
    )(psi, scales, inner, *source)


def device(chunk, block):
    return (chunk ^ ((block >> 1) & 1)) * N_BLK + block


def halos(edges):
    near, far, near_side, far_side = edges
    axes = ("inst", "blk")
    places = [(c, b) for c in range(INST) for b in range(N_BLK)]
    in_pair = [(device(c, b), device(c, b ^ 1)) for c, b in places]
    across = [
        (device(c, b), device(c, (b + 2 * (b % 2) - 1) % N_BLK)) for c, b in places]
    sides_in_pair = [(device(c, b), device(c ^ 1, b)) for c, b in places]
    sides_across = [
        (device(c, b), device(c + 2 * (c % 2) - 1, b))
        for c, b in places if 0 < c < INST - 1]
    return (
        lax.ppermute(near, axes, in_pair),
        lax.ppermute(far, axes, across),
        lax.ppermute(near_side, axes, sides_in_pair),
        lax.ppermute(far_side, axes, sides_across),
    )


def stacked(x):
    return jnp.concatenate(two_parts(x), axis=0)


def times_transposed(x, y):
    return lax.dot_general(x, y, (((1,), (1,)), ((), ())), preferred_element_type=jnp.float32)


def two_parts(x):
    a = x.astype(jnp.bfloat16)
    return a, (x - a.astype(jnp.float32)).astype(jnp.bfloat16)


def last_kernel(count, faces, most, psi, scales, a, b, c, d, list_cell, list_face,
                out, placed, *sums):
    i = pl.program_id(0)
    side = sides()
    both = [[] for f in range(F)]
    for t in range(TILES):
        scale = scales[0, t]
        for f in range(F):
            new = most[0, f * TILES + t] + scale * rim(0, t, f, side, a, b, c, d)
            out[i, f * TILES + t] = new
            both[f].append(new + psi[0, f * TILES + t])
            if t % 2:
                rows = slice((f * TILES + t - 1) * 8, (f * TILES + t + 1) * 8)
                for part, value in zip(sums, two_parts(jnp.concatenate(both[f][-2:], axis=0))):
                    part[i, rows, :] = value

    @pl.when(i == INST - 1)
    def _():
        groups = (count[0] + 127) // 128
        row = rows_iota()
        placed[...] = jnp.zeros_like(placed)

        def pick(g, carry):
            cell = list_cell[pl.ds(g, 1), :]
            onehot = (rows_iota((128, 128)) == (cell & 127)).astype(jnp.bfloat16)
            here = row == (cell >> 13)
            tile = (cell >> 7) & 7
            masks = [here & (tile == t) for t in range(TILES)]
            found = []
            for j in range(INST):
                taken = sum(
                    jnp.dot(part[j], onehot, preferred_element_type=jnp.float32) for part in sums)
                picked = jnp.zeros((8, 128), jnp.float32)
                for f in range(F):
                    total = jnp.zeros((8, 128), jnp.float32)
                    for t in range(TILES):
                        at = (f * TILES + t) * 8
                        total = jnp.where(masks[t], taken[at : at + 8, :], total)
                    total = jnp.sum(total, axis=0, keepdims=True)
                    picked = jnp.where(row == f, total, picked)
                found.append(picked)
            parts = stacked(jnp.concatenate(found, axis=0))
            face = list_face[pl.ds(g, 1), :]
            last = jnp.minimum(g * 128 + 127, count[0] - 1)

            def place(quad, carry):
                onehot = ((rows_iota((512, 128)) + quad * 512) == face).astype(jnp.bfloat16)
                total = times_transposed(parts, onehot)
                for q in range(4):
                    cols = slice(q * 128, (q + 1) * 128)
                    for j in range(INST):
                        rows = [total[n : n + 8, cols] for n in (j * 8, 64 + j * 8)]
                        at = quad * 4 + q
                        placed[j, at] = placed[j, at] + (rows[0] + rows[1])
                return carry

            lax.fori_loop(faces[g * 128] >> 9, (faces[last] >> 9) + 1, place, 0)
            return carry

        lax.fori_loop(0, groups, pick, 0)
        for j in range(INST):
            for b in range(PACKED):
                rest = pltpu.roll(placed[j, PACKED + b // 3], 6 - 2 * (b % 3), 0)
                out[j, STATE + b] = jnp.where(row < F, placed[j, b], rest)


def last_state(count, most, psi, scales, halo, list_cell, list_face):
    block = one(STATE, 8, 128)
    faces = full((GROUPS, 128))
    shape = (INST, STATE + PACKED, 8, 128)
    return pl.pallas_call(
        last_kernel,
        grid=(INST,),
        in_specs=[pl.BlockSpec(memory_space=pltpu.SMEM)] * 2 + [block, block,
                  one(2 * TILES, 8, 128)] + HALO_SPECS + [faces, faces],
        out_specs=full(shape),
        out_shape=f32(*shape),
        scratch_shapes=[pltpu.VMEM((INST, GROUPS, 8, 128), jnp.float32)]
        + [pltpu.VMEM((INST, STATE * 8, 128), jnp.bfloat16)] * 2,
        compiler_params=params(),
        cost_estimate=cost(10**8, 7 * 10**6),
    )(count, list_face, most, psi, scales, *halo, list_cell.reshape(GROUPS, 128), list_face.reshape(GROUPS, 128))


def unpack_kernel(flip, got, psi):
    for t in range(TILES):
        for f in range(F):
            psi[0, f, :, t * 128 : (t + 1) * 128] = got[0, f * TILES + t]


def unpack(got, flip):
    return pl.pallas_call(
        unpack_kernel,
        grid_spec=pltpu.PrefetchScalarGridSpec(
            num_scalar_prefetch=1,
            grid=(INST,),
            in_specs=[pl.BlockSpec((1, STATE, 8, 128), lambda d, flip: (d, 0, 0, 0))],
            out_specs=pl.BlockSpec((1, F, 8, 1024), lambda d, flip: (0, 0, 0, d ^ flip[0])),
        ),
        out_shape=f32(1, F, 8, 8192),
        compiler_params=params(),
        cost_estimate=cost(10**6, 4 * 10**6),
    )(flip, got)


def slots_kernel(got, geometry, slot, node, out):
    row = rows_iota()
    total = jnp.zeros((2 * N_BLK * 8, 128), jnp.float32)
    sums = []
    for b in range(PACKED):
        picked = got[0, b]
        for c in range(1, INST):
            picked = picked + got[c, b]
        sums.append(picked)
    for q in range(GROUPS - PACKED):
        picked = pltpu.roll(sums[3 * q], 2, 0)
        for m in (1, 2):
            rest = pltpu.roll(sums[3 * q + m], 2 + 2 * m, 0)
            picked = jnp.where((row >> 1) == m, rest, picked)
        sums.append(picked)
    for b in range(GROUPS):
        cols = slice(b * 128, (b + 1) * 128)
        picked = sums[b]
        values = jnp.broadcast_to(node[:, cols].astype(jnp.float32), (8, 128))
        for k in range(3):
            part = jnp.sum(geometry[k * F : (k + 1) * F, cols] * picked[0:F, :], axis=0, keepdims=True)
            values = jnp.where((row >> 1) == k, part, values)
        place = slot[:, cols]
        half = (row & 1) == ((place >> 7) & 1)
        owner = place >> 8
        values = jnp.where(half, values, 0.0)
        rows = jnp.concatenate(
            [jnp.where(owner == d, values, 0.0) for d in range(N_BLK)], axis=0)
        onehot = (rows_iota((128, 128)) == (place & 127)).astype(jnp.bfloat16)
        total = total + times_transposed(stacked(rows), onehot)
    total = total[0:128] + total[128:256]
    for i in range(INST):
        for d in range(N_BLK):
            out[i * N_BLK + d] = total[d * 8 : d * 8 + 8, :]


def pack_slots(got, geometry, slot, node):
    return pl.pallas_call(
        slots_kernel,
        grid=(1,),
        in_specs=[pl.BlockSpec((INST, PACKED, 8, 128), lambda _: (0, STATE // PACKED, 0, 0)),
                  full((3 * F, FACES)), full((1, FACES)), full((1, FACES))],
        out_specs=full((INST * N_BLK, 8, 128)),
        out_shape=f32(INST * N_BLK, 8, 128),
        compiler_params=params(),
        cost_estimate=cost(10**8, 2 * 10**6),
    )(got, geometry, slot.reshape(1, FACES), node.reshape(1, FACES))


def nodes_kernel(got, out):
    total = jnp.zeros((2 * 96, 128), jnp.float32)
    for b in range(N_BLK):
        values = got[b]
        for i in range(1, INST):
            values = values + got[i * N_BLK + b]
        nodes = got[b].astype(jnp.int32)
        for half in range(2):
            node = nodes[6 + half : 7 + half, :]
            high = rows_iota((32, 128)) == (node >> 7)
            rows = jnp.concatenate(
                [jnp.where(high, values[k * 2 + half : k * 2 + half + 1, :], 0.0) for k in range(3)],
                axis=0)
            onehot = (rows_iota((128, 128)) == (node & 127)).astype(jnp.bfloat16)
            total = total + times_transposed(stacked(rows), onehot)
    total = total[0:96] + total[96:192]
    for k in range(3):
        for h in range(32):
            out[k : k + 1, h * 128 : (h + 1) * 128] = total[k * 32 + h : k * 32 + h + 1, :]


def to_nodes(got):
    return pl.pallas_call(
        nodes_kernel,
        in_specs=[pl.BlockSpec(memory_space=pltpu.VMEM)],
        out_specs=pl.BlockSpec(memory_space=pltpu.VMEM),
        out_shape=f32(3, NODE_DEV),
        compiler_params=params(),
        cost_estimate=cost(10**8, 10**6),
    )(got)


def local(psi_start, coupling, center, spread, source, wall_geo, wall_cell, wall_dest, wall_node):
    block = lax.axis_index("blk").astype(jnp.int32)
    flip = ((block >> 1) & 1).reshape(1)
    chunk = lax.axis_index("inst").astype(jnp.int32).reshape(1) ^ flip

    got = lax.all_to_all(
        pack(psi_start[0], center[0], spread[0], coupling), "inst", 0, 0, tiled=True)
    faces = sort_faces(wall_cell, wall_dest[:, 0], chunk)
    sent = pack_source(source[0])
    got, sent, (list_cell, list_face, slot, count) = lax.optimization_barrier((got, sent, faces))
    got_source = lax.all_to_all(sent, "inst", 0, 0, tiled=True)

    inner, *edges, psi, scales = first_fluxes(got)
    halo = halos(edges)
    most = most_of_sweep(psi, scales, inner)
    psi, source, inner, *edges = second_fluxes(got_source, most, scales, halo)
    halo = halos(edges)
    most = most_of_sweep(psi, scales, inner, source)
    back = last_state(count, most, psi, scales, halo, list_cell, list_face)

    home = lax.all_to_all(back, "inst", 0, 0, tiled=True)
    slots = pack_slots(home, wall_geo[0], slot, wall_node)
    owned = lax.all_to_all(slots, ("inst", "blk"), 0, 0, tiled=True)
    return unpack(home, flip), to_nodes(owned)


def solution(mesh):
    placed = (
        P("inst", None, "blk", None),
        P("inst", None, None),
        P("inst", "blk", None),
        P("inst", "blk", None),
        P("inst", None, "blk", None),
        P("inst", None, "blk"),
        P("blk"),
        P("blk", None),
        P("blk"),
    )
    return jax.shard_map(
        local,
        mesh=mesh,
        in_specs=placed,
        out_specs=(P("inst", None, "blk", None), P(None, "blk")),
        check_vma=False,
    )
```

```python
import math

import jax
import jax.numpy as jnp
from jax import lax
from jax.experimental import pallas as pl
from jax.experimental.pallas import tpu as pltpu
from jax.sharding import PartitionSpec as P

CAP = 256
NODE_DEV = 4096
INST = 8
N_BLK = 16
F = 6
TILES = 8
FACES = 2048
GROUPS = FACES // 128
PACKED = GROUPS * F // 8
VMEM = 16 * 1024 * 1024
STATE = F * TILES
SENT = STATE + 2 * TILES + 1

HALF_SPEC = [0.0] + [
    0.25 * (-1.0) ** d / math.sin(math.pi * d / INST) for d in range(1, INST)
]


def params(limit=VMEM):
    return pltpu.CompilerParams(vmem_limit_bytes=limit)


def cost(flops, nbytes):
    return pl.CostEstimate(flops=flops, bytes_accessed=nbytes, transcendentals=0)


def rows_iota(shape=(8, 128)):
    return lax.broadcasted_iota(jnp.int32, shape, 0)


def lanes_iota(shape=(8, 128)):
    return lax.broadcasted_iota(jnp.int32, shape, 1)


def full(shape):
    return pl.BlockSpec(shape, lambda *_: (0,) * len(shape))


def one(*shape):
    return pl.BlockSpec((1,) + shape, lambda i: (i,) + (0,) * len(shape))


def f32(*shape):
    return jax.ShapeDtypeStruct(shape, jnp.float32)


def tiled(x):
    x = x.reshape(x.shape[:-1] + (INST * TILES, 128))
    return jnp.swapaxes(x, -3, -2)


def flipped():
    return (lax.axis_index("blk").astype(jnp.int32) >> 1) & 1


def sides():
    chunk = lax.axis_index("inst").astype(jnp.int32) ^ flipped()
    return lax.axis_index("blk").astype(jnp.int32) & 1, chunk & 1


def tiles_of(d, flip):
    return pl.ds((d ^ flip) * TILES, TILES)


def pack_kernel(psi, center, spread, coupling, out, flat, factors, held, sems, more):
    flip = flipped()

    def load(d):
        state = held.at[d, pl.ds(0, STATE)].reshape(F, TILES, 8, 128)
        return pltpu.make_async_copy(psi.at[:, tiles_of(d, flip)], state, sems.at[d])

    def send(d):
        return pltpu.make_async_copy(held.at[d], out.at[d], more.at[2 + d])

    flats = [
        pltpu.make_async_copy(coupling, factors, more.at[2 + INST]),
        pltpu.make_async_copy(center, flat.at[0], more.at[0]),
        pltpu.make_async_copy(spread, flat.at[1], more.at[1]),
    ]
    for copy in flats:
        copy.start()
    for d in range(INST):
        load(d).start()
    for copy in flats:
        copy.wait()
    for d in range(INST):
        held[d, STATE : STATE + TILES] = 0.6 / flat[0, tiles_of(d, flip)]
        held[d, STATE + TILES : STATE + 2 * TILES] = flat[1, tiles_of(d, flip)]
        held[d, SENT - 1] = jnp.zeros((8, 128), jnp.float32)
        for g in range(F):
            held[d, SENT - 1, g : g + 1, 0:F] = factors[g]
        load(d).wait()
        send(d).start()
    for d in range(INST):
        send(d).wait()


def pack(psi, center, spread, coupling):
    anywhere = pl.BlockSpec(memory_space=pl.ANY)
    return pl.pallas_call(
        pack_kernel,
        in_specs=[anywhere] * 4,
        out_specs=anywhere,
        out_shape=f32(INST, SENT, 8, 128),
        scratch_shapes=[
            pltpu.VMEM((2, INST * TILES, 8, 128), jnp.float32),
            pltpu.VMEM((F, 1, F), jnp.float32),
            pltpu.VMEM((INST, SENT, 8, 128), jnp.float32),
            pltpu.SemaphoreType.DMA((INST,)),
            pltpu.SemaphoreType.DMA((3 + INST,)),
        ],
        compiler_params=params(60 * 1024 * 1024),
        cost_estimate=cost(10**6, 5 * 10**6),
    )(tiled(psi), tiled(center), tiled(spread), jnp.swapaxes(coupling, 0, 1))


def pack_source_kernel(source, out, held, sems, more):
    flip = flipped()

    def load(d, f):
        start = source.at[f, tiles_of(d, flip)]
        return pltpu.make_async_copy(start, held.at[d, pl.ds(f * TILES, TILES)], sems.at[d, f])

    def send(d):
        return pltpu.make_async_copy(held.at[d], out.at[d], more.at[d])

    for d in range(INST):
        for f in range(F):
            load(d, f).start()
    for d in range(INST):
        for f in range(F):
            load(d, f).wait()
        send(d).start()
    for d in range(INST):
        send(d).wait()


def pack_source(source):
    anywhere = pl.BlockSpec(memory_space=pl.ANY)
    return pl.pallas_call(
        pack_source_kernel,
        in_specs=[anywhere],
        out_specs=anywhere,
        out_shape=f32(INST, STATE, 8, 128),
        scratch_shapes=[
            pltpu.VMEM((INST, STATE, 8, 128), jnp.float32),
            pltpu.SemaphoreType.DMA((INST, F)),
            pltpu.SemaphoreType.DMA((INST,)),
        ],
        compiler_params=params(60 * 1024 * 1024),
        cost_estimate=cost(10**6, 4 * 10**6),
    )(tiled(source))


def faces_kernel(cell, dest, chunk, list_cell, list_face, slot, count, loads):
    for owner in range(N_BLK):
        loads[owner] = 0

    def step(face, found):
        here = cell[face]
        owner = dest[face]
        rank = loads[owner]
        slot[face] = owner * CAP + rank
        loads[owner] = rank + 1
        list_cell[found] = here
        list_face[found] = face
        mine = ((here & 8191) >> 10) == chunk[0]
        return found + mine.astype(jnp.int32)

    found = lax.fori_loop(0, FACES, step, jnp.int32(0))
    count[0] = found

    def fill(at, carry):
        list_cell[at] = 0
        list_face[at] = -1
        return carry

    lax.fori_loop(found, jnp.minimum(found + 128, FACES), fill, 0)


def sort_faces(cell, dest, chunk):
    smem = pl.BlockSpec(memory_space=pltpu.SMEM)
    ints = jax.ShapeDtypeStruct((FACES,), jnp.int32)
    return pl.pallas_call(
        faces_kernel,
        in_specs=[smem] * 3,
        out_specs=[smem] * 4,
        out_shape=[ints, ints, ints, jax.ShapeDtypeStruct((1,), jnp.int32)],
        scratch_shapes=[pltpu.SMEM((N_BLK,), jnp.int32)],
        compiler_params=pltpu.CompilerParams(vmem_limit_bytes=2**20),
        cost_estimate=cost(10**9, 10**7),
    )(cell, dest, chunk)


def fluxes(i, side, psi_of, spread_of, coupling, inner, near, far, near_side, far_side, held):
    row, lane = rows_iota(), lanes_iota()
    factor = [
        [jnp.broadcast_to(coupling[g : g + 1, f : f + 1], (8, 128)) for f in range(F)]
        for g in range(F)
    ]
    for t in range(TILES):
        psi = [psi_of(t, f) for f in range(F)]
        strength = spread_of(t)
        for f in range(F):
            total = factor[0][f] * psi[0]
            for g in range(1, F):
                total = total + factor[g][f] * psi[g]
            weighted = strength * total
            at = (f * TILES + t) * 8
            held[at : at + 8, :] = weighted
    near_row = jnp.where(side[0] == 1, 0, 7)
    first = jnp.zeros((8, 128), jnp.float32)
    last = jnp.zeros((8, 128), jnp.float32)
    for f in range(F):
        near[i, f] = held[pl.ds(f * TILES * 8 + near_row, TILES, stride=8), :]
        far[i, f] = held[pl.ds(f * TILES * 8 + 7 - near_row, TILES, stride=8), :]
        tiles = [held[(f * TILES + t) * 8 : (f * TILES + t + 1) * 8, :] for t in range(TILES)]
        later = [pltpu.roll(x, 1, 1) for x in tiles]
        sooner = [pltpu.roll(x, 127, 1) for x in tiles]
        first = jnp.where(lane == f, jnp.broadcast_to(tiles[0][:, 0:1], (8, 128)), first)
        last = jnp.where(lane == f, jnp.broadcast_to(tiles[7][:, 127:128], (8, 128)), last)
        for t in range(TILES):
            before = later[t - 1] if t else jnp.zeros((8, 128), jnp.float32)
            after = sooner[t + 1] if t < TILES - 1 else jnp.zeros((8, 128), jnp.float32)
            total = jnp.where(lane == 0, before, later[t])
            total = total + jnp.where(lane == 127, after, sooner[t])
            total = total + jnp.where(row == 0, 0.0, pltpu.roll(tiles[t], 1, 0))
            total = total + jnp.where(row == 7, 0.0, pltpu.roll(tiles[t], 7, 0))
            inner[i, f * TILES + t] = total
    near_side[i] = jnp.where(side[1] == 1, first, last)
    far_side[i] = jnp.where(side[1] == 1, last, first)


FLUX_SHAPES = [
    f32(INST, STATE, 8, 128),
    f32(INST, F, 8, 128),
    f32(INST, F, 8, 128),
    f32(INST, 8, 128),
    f32(INST, 8, 128),
]


def first_kernel(got, inner, near, far, near_side, far_side, psi, scales, held, sems):
    side = sides()

    def loads(i, n):
        to = (psi, scales)[n]
        start = got.at[i, pl.ds(n * STATE, to.shape[1])]
        return pltpu.make_async_copy(start, to.at[i], sems.at[n, i])

    for i in range(INST):
        loads(i, 0).start()
        loads(i, 1).start()

    def step(i, carry):
        loads(i, 0).wait()
        loads(i, 1).wait()
        fluxes(
            i, side,
            lambda t, f: psi[i, f * TILES + t],
            lambda t: scales[i, TILES + t],
            scales[i, 2 * TILES],
            inner, near, far, near_side, far_side, held,
        )
        return carry

    lax.fori_loop(0, INST, step, 0)


def first_fluxes(got):
    vmem = pl.BlockSpec(memory_space=pltpu.VMEM)
    return pl.pallas_call(
        first_kernel,
        in_specs=[pl.BlockSpec(memory_space=pl.ANY)],
        out_specs=[vmem] * 7,
        out_shape=FLUX_SHAPES + [f32(INST, STATE, 8, 128), f32(INST, 2 * TILES + 1, 8, 128)],
        scratch_shapes=[
            pltpu.VMEM((STATE * 8, 128), jnp.float32),
            pltpu.SemaphoreType.DMA((2, INST)),
        ],
        compiler_params=params(),
        cost_estimate=cost(10**7, 7 * 10**6),
    )(got)


def rim(i, t, f, side, near, far, near_side, far_side):
    row, lane = rows_iota(), lanes_iota()
    near_row = jnp.where(side[0] == 1, 0, 7)
    total = jnp.where(row == near_row, near[i, f, t : t + 1, :], 0.0)
    total = total + jnp.where(row == 7 - near_row, far[i, f, t : t + 1, :], 0.0)
    if t == 0:
        left = jnp.where(side[1] == 1, near_side[i], far_side[i])
        total = total + jnp.where(lane == 0, jnp.broadcast_to(left[:, f : f + 1], (8, 128)), 0.0)
    if t == TILES - 1:
        right = jnp.where(side[1] == 1, far_side[i], near_side[i])
        total = total + jnp.where(lane == 127, jnp.broadcast_to(right[:, f : f + 1], (8, 128)), 0.0)
    return total


def second_kernel(got, most, scales, a, b, c, d,
                  psi, source, inner, near, far, near_side, far_side, held, sems):
    side = sides()

    def load(i):
        return pltpu.make_async_copy(got.at[i], source.at[i], sems.at[i])

    for i in range(2):
        load(i).start()

    def step(i, carry):
        load(i).wait()

        @pl.when(i + 2 < INST)
        def _():
            load(i + 2).start()

        for t in range(TILES):
            scale = scales[i, t]
            for f in range(F):
                at = f * TILES + t
                psi[i, at] = most[i, at] + scale * (source[i, at] + rim(i, t, f, side, a, b, c, d))
        fluxes(
            i, side,
            lambda t, f: psi[i, f * TILES + t],
            lambda t: scales[i, TILES + t],
            scales[i, 2 * TILES],
            inner, near, far, near_side, far_side, held,
        )
        return carry

    lax.fori_loop(0, INST, step, 0)


HALO_SPECS = [one(F, 8, 128), one(F, 8, 128), one(8, 128), one(8, 128)]


def second_fluxes(got, most, scales, halo):
    vmem = pl.BlockSpec(memory_space=pltpu.VMEM)
    state = f32(INST, STATE, 8, 128)
    return pl.pallas_call(
        second_kernel,
        in_specs=[pl.BlockSpec(memory_space=pl.ANY)] + [vmem] * 6,
        out_specs=[vmem] * 7,
        out_shape=[state, state] + FLUX_SHAPES,
        scratch_shapes=[
            pltpu.VMEM((STATE * 8, 128), jnp.float32),
            pltpu.SemaphoreType.DMA((INST,)),
        ],
        compiler_params=params(),
        cost_estimate=cost(10**7, 7 * 10**6),
    )(got, most, scales, *halo)


def spectral(psi):
    def at(j):
        return (psi[j], 1) if j < INST else (psi[j - INST], -1)

    totals = []
    for i in range(INST):
        total = None
        for d in (1, 2, 3):
            (x, p), (y, q) = at(i + d), at(i + INST - d)
            pair = x + y if p == q else x - y
            sign = p
            term = (sign * HALF_SPEC[d]) * pair
            total = term if total is None else total + term
        x, p = at(i + 4)
        totals.append(total + (p * HALF_SPEC[4]) * x)
    return totals


def most_kernel(psi, scale, inner, *rest):
    most = rest[-1]
    for t in range(TILES):
        state = [psi[i, t] for i in range(INST)]
        coupled = spectral(state)
        for i in range(INST):
            change = inner[i, t] - coupled[i]
            if len(rest) > 1:
                change = change + rest[0][i, t]
            most[i, t] = 0.4 * state[i] + scale[i, t] * change


def most_of_sweep(psi, scales, inner, *source):
    field = pl.BlockSpec((INST, TILES, 8, 128), lambda f: (0, f, 0, 0))
    scale = pl.BlockSpec((INST, TILES, 8, 128), lambda f: (0, 0, 0, 0))
    return pl.pallas_call(
        most_kernel,
        grid=(F,),
        in_specs=[field, scale, field] + [field] * len(source),
        out_specs=field,
        out_shape=f32(INST, STATE, 8, 128),
        compiler_params=params(),
        cost_estimate=cost(10**7, 8 * 10**6),
    )(psi, scales, inner, *source)


def device(chunk, block):
    return (chunk ^ ((block >> 1) & 1)) * N_BLK + block


def halos(edges):
    near, far, near_side, far_side = edges
    axes = ("inst", "blk")
    places = [(c, b) for c in range(INST) for b in range(N_BLK)]
    in_pair = [(device(c, b), device(c, b ^ 1)) for c, b in places]
    across = [
        (device(c, b), device(c, (b + 2 * (b % 2) - 1) % N_BLK)) for c, b in places]
    sides_in_pair = [(device(c, b), device(c ^ 1, b)) for c, b in places]
    sides_across = [
        (device(c, b), device(c + 2 * (c % 2) - 1, b))
        for c, b in places if 0 < c < INST - 1]
    return (
        lax.ppermute(near, axes, in_pair),
        lax.ppermute(far, axes, across),
        lax.ppermute(near_side, axes, sides_in_pair),
        lax.ppermute(far_side, axes, sides_across),
    )


def stacked(x):
    return jnp.concatenate(two_parts(x), axis=0)


def times_transposed(x, y):
    return lax.dot_general(x, y, (((1,), (1,)), ((), ())), preferred_element_type=jnp.float32)


def two_parts(x):
    a = x.astype(jnp.bfloat16)
    return a, (x - a.astype(jnp.float32)).astype(jnp.bfloat16)


def last_kernel(count, faces, most, psi, scales, a, b, c, d, list_cell, list_face,
                out, placed, *sums):
    i = pl.program_id(0)
    side = sides()
    both = [[] for f in range(F)]
    for t in range(TILES):
        scale = scales[0, t]
        for f in range(F):
            new = most[0, f * TILES + t] + scale * rim(0, t, f, side, a, b, c, d)
            out[i, f * TILES + t] = new
            both[f].append(new + psi[0, f * TILES + t])
            if t % 2:
                rows = slice((f * TILES + t - 1) * 8, (f * TILES + t + 1) * 8)
                for part, value in zip(sums, two_parts(jnp.concatenate(both[f][-2:], axis=0))):
                    part[i, rows, :] = value

    @pl.when(i == INST - 1)
    def _():
        groups = (count[0] + 127) // 128
        row = rows_iota()
        placed[...] = jnp.zeros_like(placed)

        def pick(g, carry):
            cell = list_cell[pl.ds(g, 1), :]
            onehot = (rows_iota((128, 128)) == (cell & 127)).astype(jnp.bfloat16)
            here = row == (cell >> 13)
            tile = (cell >> 7) & 7
            masks = [here & (tile == t) for t in range(TILES)]
            found = []
            for j in range(INST):
                taken = sum(
                    jnp.dot(part[j], onehot, preferred_element_type=jnp.float32) for part in sums)
                picked = jnp.zeros((8, 128), jnp.float32)
                for f in range(F):
                    total = jnp.zeros((8, 128), jnp.float32)
                    for t in range(TILES):
                        at = (f * TILES + t) * 8
                        total = jnp.where(masks[t], taken[at : at + 8, :], total)
                    total = jnp.sum(total, axis=0, keepdims=True)
                    picked = jnp.where(row == f, total, picked)
                found.append(picked)
            parts = stacked(jnp.concatenate(found, axis=0))
            face = list_face[pl.ds(g, 1), :]
            last = jnp.minimum(g * 128 + 127, count[0] - 1)

            def place(quad, carry):
                onehot = ((rows_iota((512, 128)) + quad * 512) == face).astype(jnp.bfloat16)
                total = times_transposed(parts, onehot)
                for q in range(4):
                    cols = slice(q * 128, (q + 1) * 128)
                    for j in range(INST):
                        rows = [total[n : n + 8, cols] for n in (j * 8, 64 + j * 8)]
                        at = quad * 4 + q
                        placed[j, at] = placed[j, at] + (rows[0] + rows[1])
                return carry

            lax.fori_loop(faces[g * 128] >> 9, (faces[last] >> 9) + 1, place, 0)
            return carry

        lax.fori_loop(0, groups, pick, 0)
        for j in range(INST):
            for b in range(PACKED):
                rest = pltpu.roll(placed[j, PACKED + b // 3], 6 - 2 * (b % 3), 0)
                out[j, STATE + b] = jnp.where(row < F, placed[j, b], rest)


def last_state(count, most, psi, scales, halo, list_cell, list_face):
    block = one(STATE, 8, 128)
    faces = full((GROUPS, 128))
    shape = (INST, STATE + PACKED, 8, 128)
    return pl.pallas_call(
        last_kernel,
        grid=(INST,),
        in_specs=[pl.BlockSpec(memory_space=pltpu.SMEM)] * 2 + [block, block,
                  one(2 * TILES, 8, 128)] + HALO_SPECS + [faces, faces],
        out_specs=full(shape),
        out_shape=f32(*shape),
        scratch_shapes=[pltpu.VMEM((INST, GROUPS, 8, 128), jnp.float32)]
        + [pltpu.VMEM((INST, STATE * 8, 128), jnp.bfloat16)] * 2,
        compiler_params=params(),
        cost_estimate=cost(10**8, 7 * 10**6),
    )(count, list_face, most, psi, scales, *halo, list_cell.reshape(GROUPS, 128), list_face.reshape(GROUPS, 128))


def unpack_kernel(flip, got, psi):
    for t in range(TILES):
        for f in range(F):
            psi[0, f, :, t * 128 : (t + 1) * 128] = got[0, f * TILES + t]


def unpack(got, flip):
    return pl.pallas_call(
        unpack_kernel,
        grid_spec=pltpu.PrefetchScalarGridSpec(
            num_scalar_prefetch=1,
            grid=(INST,),
            in_specs=[pl.BlockSpec((1, STATE, 8, 128), lambda d, flip: (d, 0, 0, 0))],
            out_specs=pl.BlockSpec((1, F, 8, 1024), lambda d, flip: (0, 0, 0, d ^ flip[0])),
        ),
        out_shape=f32(1, F, 8, 8192),
        compiler_params=params(),
        cost_estimate=cost(10**6, 4 * 10**6),
    )(flip, got)


def slots_kernel(got, geometry, slot, node, out):
    row = rows_iota()
    total = jnp.zeros((2 * N_BLK * 8, 128), jnp.float32)
    sums = []
    for b in range(PACKED):
        picked = got[0, b]
        for c in range(1, INST):
            picked = picked + got[c, b]
        sums.append(picked)
    for q in range(GROUPS - PACKED):
        picked = pltpu.roll(sums[3 * q], 2, 0)
        for m in (1, 2):
            rest = pltpu.roll(sums[3 * q + m], 2 + 2 * m, 0)
            picked = jnp.where((row >> 1) == m, rest, picked)
        sums.append(picked)
    for b in range(GROUPS):
        cols = slice(b * 128, (b + 1) * 128)
        picked = sums[b]
        values = jnp.broadcast_to(node[:, cols].astype(jnp.float32), (8, 128))
        for k in range(3):
            part = jnp.sum(geometry[k * F : (k + 1) * F, cols] * picked[0:F, :], axis=0, keepdims=True)
            values = jnp.where((row >> 1) == k, part, values)
        place = slot[:, cols]
        half = (row & 1) == ((place >> 7) & 1)
        owner = place >> 8
        values = jnp.where(half, values, 0.0)
        rows = jnp.concatenate(
            [jnp.where(owner == d, values, 0.0) for d in range(N_BLK)], axis=0)
        onehot = (rows_iota((128, 128)) == (place & 127)).astype(jnp.bfloat16)
        total = total + times_transposed(stacked(rows), onehot)
    total = total[0:128] + total[128:256]
    for i in range(INST):
        for d in range(N_BLK):
            out[i * N_BLK + d] = total[d * 8 : d * 8 + 8, :]


def pack_slots(got, geometry, slot, node):
    return pl.pallas_call(
        slots_kernel,
        grid=(1,),
        in_specs=[pl.BlockSpec((INST, PACKED, 8, 128), lambda _: (0, STATE // PACKED, 0, 0)),
                  full((3 * F, FACES)), full((1, FACES)), full((1, FACES))],
        out_specs=full((INST * N_BLK, 8, 128)),
        out_shape=f32(INST * N_BLK, 8, 128),
        compiler_params=params(),
        cost_estimate=cost(10**8, 2 * 10**6),
    )(got, geometry, slot.reshape(1, FACES), node.reshape(1, FACES))


def nodes_kernel(got, out):
    total = jnp.zeros((2 * 96, 128), jnp.float32)
    for b in range(N_BLK):
        values = got[b]
        for i in range(1, INST):
            values = values + got[i * N_BLK + b]
        nodes = got[b].astype(jnp.int32)
        for half in range(2):
            node = nodes[6 + half : 7 + half, :]
            high = rows_iota((32, 128)) == (node >> 7)
            rows = jnp.concatenate(
                [jnp.where(high, values[k * 2 + half : k * 2 + half + 1, :], 0.0) for k in range(3)],
                axis=0)
            onehot = (rows_iota((128, 128)) == (node & 127)).astype(jnp.bfloat16)
            total = total + times_transposed(stacked(rows), onehot)
    total = total[0:96] + total[96:192]
    for k in range(3):
        for h in range(32):
            out[k : k + 1, h * 128 : (h + 1) * 128] = total[k * 32 + h : k * 32 + h + 1, :]


def to_nodes(got):
    return pl.pallas_call(
        nodes_kernel,
        in_specs=[pl.BlockSpec(memory_space=pltpu.VMEM)],
        out_specs=pl.BlockSpec(memory_space=pltpu.VMEM),
        out_shape=f32(3, NODE_DEV),
        compiler_params=params(),
        cost_estimate=cost(10**8, 10**6),
    )(got)


def local(psi_start, coupling, center, spread, source, wall_geo, wall_cell, wall_dest, wall_node):
    block = lax.axis_index("blk").astype(jnp.int32)
    flip = ((block >> 1) & 1).reshape(1)
    chunk = lax.axis_index("inst").astype(jnp.int32).reshape(1) ^ flip

    got = lax.all_to_all(
        pack(psi_start[0], center[0], spread[0], coupling), "inst", 0, 0, tiled=True)
    faces = sort_faces(wall_cell, wall_dest[:, 0], chunk)
    sent = pack_source(source[0])
    got, sent, (list_cell, list_face, slot, count) = lax.optimization_barrier((got, sent, faces))
    got_source = lax.all_to_all(sent, "inst", 0, 0, tiled=True)

    inner, *edges, psi, scales = first_fluxes(got)
    halo = halos(edges)
    most = most_of_sweep(psi, scales, inner)
    psi, source, inner, *edges = second_fluxes(got_source, most, scales, halo)
    halo = halos(edges)
    most = most_of_sweep(psi, scales, inner, source)
    back = last_state(count, most, psi, scales, halo, list_cell, list_face)

    home = lax.all_to_all(back, "inst", 0, 0, tiled=True)
    slots = pack_slots(home, wall_geo[0], slot, wall_node)
    owned = lax.all_to_all(slots, ("inst", "blk"), 0, 0, tiled=True)
    return unpack(home, flip), to_nodes(owned)


def solution(mesh):
    placed = (
        P("inst", None, "blk", None),
        P("inst", None, None),
        P("inst", "blk", None),
        P("inst", "blk", None),
        P("inst", None, "blk", None),
        P("inst", None, "blk"),
        P("blk"),
        P("blk", None),
        P("blk"),
    )
    return jax.shard_map(
        local,
        mesh=mesh,
        in_specs=placed,
        out_specs=(P("inst", None, "blk", None), P(None, "blk")),
        check_vma=False,
    )
```
